256 devices in a mesh: dom: 64 (over z, x, core), grp: 4 (over y).
Axes of the slice: x: 4, y: 4, z: 8, core: 2. Of those that a mesh axis runs over, the one named last changes fastest.
Arguments:
- initial: bfloat16 [4, 32768, 512], P('grp', 'dom'), may hold values from -6 to 6
- history: bfloat16 [4, 32768, 512], P('grp', 'dom'), may hold values from 0 to 2
- tile_values: bfloat16 [4, 256, 8, 128, 128], P('grp', 'dom'), may hold values from -0.1875 to 0.1875
- tile_cols: int32 [4, 256, 8], P('grp', 'dom'), may hold values from 0 to 67
- send_blocks: int32 [4, 64, 64], P('grp', 'dom'), may hold values from 0 to 3
- weight_one: bfloat16 [512, 512], replicated, may hold values from -0.25 to 0.25
- weight_two: bfloat16 [512, 512], replicated, may hold values from -0.25 to 0.25
- cotangent: bfloat16 [4, 32768, 512], P('grp', 'dom'), may hold values from -6 to 6
Outputs:
- embeddings: bfloat16 [4, 32768, 512], P('grp', 'dom')
- grad_one: float32 [512, 512], replicated
- grad_two: float32 [512, 512], replicated
The draws below stay inside these ranges and needn't reach their ends.
All inputs are finite; a program needn't handle non-finite values.
Results may differ from the reference program's by a relative error of at most 0.0071.
Values may be sent and summed in bfloat16 or wider, within the bound.
A program may use at most 128 MiB of HBM per device.

```python
import jax
import jax.numpy as jnp
from jax import lax

D = 512
BS = 128
K = 8
NB = 4
ROWBLOCKS = 256
NODES = 32768
N_DOM = 64
N_GRP = 4


def plant(values, stream_key, smallest, largest):
    longest = values.shape.index(max(values.shape))
    spots = []
    for shift in (0, 1):
        where = [jax.random.randint(jax.random.fold_in(stream_key, axis), (), 0, length) for axis, length in enumerate(values.shape)]
        where[longest] = (where[longest] + shift) % values.shape[longest]
        spots.append(tuple(where))
    return values.at[spots[0]].set(smallest).at[spots[1]].set(largest)


def levels(own_key, extent, split, low, high):
    def one(position, blocks):
        heights = jax.random.uniform(jax.random.fold_in(jax.random.fold_in(own_key, 6), position), (blocks,), jnp.float32, low / len(split), high / len(split))
        return jnp.repeat(jnp.exp(heights), extent[position] // blocks).reshape((-1,) + (1,) * (len(extent) - position - 1))

    gain = one(*split[0])
    for cut in split[1:]:
        gain = gain * one(*cut)
    return gain


def scatter_about(key, shape, scale, reach, split=(), kind=jnp.bfloat16):
    gain = levels(key, shape, split, -0.22, 0.18) if split else 1.0
    result = jax.random.normal(key, shape, jnp.float32) * scale * gain
    return jnp.minimum(jnp.maximum(result, -reach), reach).astype(kind)


def setup_inputs(seed: int = 0) -> dict:
    key_of = jax.random.split(jax.random.key(seed), 9)
    initial = scatter_about(key_of[0], (N_GRP, NODES, D), 1.0, 6.0, ((0, 4), (1, 64)))
    history = jnp.clip(2.0 * jax.random.uniform(key_of[1], (N_GRP, NODES, D), jnp.float32) ** levels(key_of[1], (N_GRP, NODES, D), ((0, 4), (1, 64)), -0.2, 0.2), 0.0, 2.0).astype(jnp.bfloat16)
    tile_values = scatter_about(key_of[2], (N_GRP, ROWBLOCKS, K, BS, BS), (K * BS) ** -0.5, 0.1875, ((0, 4), (1, 64)))
    tile_cols = plant(jax.random.randint(key_of[3], (N_GRP, ROWBLOCKS, K), 0, NB + N_DOM), jax.random.fold_in(key_of[3], 1), 0, (NB + N_DOM) - 1).astype(jnp.int32)
    send_blocks = plant(jax.random.randint(key_of[4], (N_GRP, N_DOM, N_DOM), 0, NB), jax.random.fold_in(key_of[4], 1), 0, NB - 1).astype(jnp.int32)
    weight_one = scatter_about(key_of[5], (D, D), D ** -0.5, 0.25)
    weight_two = scatter_about(key_of[6], (D, D), D ** -0.5, 0.25)
    cotangent = scatter_about(key_of[7], (N_GRP, NODES, D), 1.0, 6.0, ((0, 4), (1, 64)))
    return {"initial": initial, "history": history, "tile_values": tile_values, "tile_cols": tile_cols, "send_blocks": send_blocks, "weight_one": weight_one, "weight_two": weight_two, "cotangent": cotangent}


RESTART = 0.1
BETA_ONE = 0.405465
BETA_TWO = 0.223144


def silu_slope(value):
    sig = jax.nn.sigmoid(value)
    return sig * (1.0 + value * (1.0 - sig))


def propagate(tile_part, col_part, own_blocks, received):
    buffer = jnp.concatenate([own_blocks, received], axis=0)
    picked = buffer[col_part]
    return jnp.einsum("rkij,rkjd->rid", tile_part.astype(jnp.float32), picked.astype(jnp.float32))


def reader_pass(tile_part, col_part, own_flat, received_in, received_past, weight_one, weight_two, cot_flat):
    count = tile_part.shape[0]
    size = tile_part.shape[2]
    width = own_flat.shape[1]
    own_blocks = own_flat.reshape(count, size, width)
    mixed_one = ((1.0 - RESTART) * propagate(tile_part, col_part, own_blocks, received_in) + RESTART * own_blocks.astype(jnp.float32)).astype(jnp.bfloat16)
    flat_one = mixed_one.reshape(count * size, width)
    pre_one = (1.0 - BETA_ONE) * flat_one.astype(jnp.float32) + BETA_ONE * jnp.dot(flat_one, weight_one, preferred_element_type=jnp.float32)
    hidden_one = jax.nn.silu(pre_one).astype(jnp.bfloat16)
    mixed_two = ((1.0 - RESTART) * propagate(tile_part, col_part, hidden_one.reshape(count, size, width), received_past) + RESTART * own_blocks.astype(jnp.float32)).astype(jnp.bfloat16)
    flat_two = mixed_two.reshape(count * size, width)
    pre_two = (1.0 - BETA_TWO) * flat_two.astype(jnp.float32) + BETA_TWO * jnp.dot(flat_two, weight_two, preferred_element_type=jnp.float32)
    output = jax.nn.silu(pre_two).astype(jnp.bfloat16)
    back_two = (cot_flat.astype(jnp.float32) * silu_slope(pre_two)).astype(jnp.bfloat16)
    grad_two = BETA_TWO * jnp.einsum("nd,ne->de", flat_two.astype(jnp.float32), back_two.astype(jnp.float32))
    back_mixed = ((1.0 - BETA_TWO) * back_two.astype(jnp.float32) + BETA_TWO * jnp.dot(back_two, weight_two.T, preferred_element_type=jnp.float32)).astype(jnp.bfloat16)
    pieces = jnp.einsum("rkij,rid->rkjd", tile_part.astype(jnp.float32), back_mixed.reshape(count, size, width).astype(jnp.float32))
    selector = (col_part[None, :, :] == jnp.arange(count, dtype=jnp.int32)[:, None, None]).astype(jnp.float32)
    back_hidden = (1.0 - RESTART) * jnp.einsum("crk,rkjd->cjd", selector, pieces)
    back_one = (back_hidden.reshape(count * size, width) * silu_slope(pre_one)).astype(jnp.bfloat16)
    grad_one = BETA_ONE * jnp.einsum("nd,ne->de", flat_one.astype(jnp.float32), back_one.astype(jnp.float32))
    return output, grad_one, grad_two


def reference(initial, history, tile_values, tile_cols, send_blocks, weight_one, weight_two, cotangent):
    width = initial.shape[2]
    init_blocks = initial.reshape(N_GRP, N_DOM, NB, BS, width)
    past_blocks = history.reshape(N_GRP, N_DOM, NB, BS, width)
    tiles_all = tile_values.reshape(N_GRP * N_DOM, NB, K, BS, BS)
    cols_all = tile_cols.reshape(N_GRP * N_DOM, NB, K)
    own_all = initial.reshape(N_GRP * N_DOM, NB * BS, width)
    cot_all = cotangent.reshape(N_GRP * N_DOM, NB * BS, width)
    owners = jnp.arange(N_DOM, dtype=jnp.int32)

    def step(carry, inputs):
        tile_part, col_part, own_flat, cot_flat, index = inputs
        group = index // N_DOM
        reader = index % N_DOM
        chosen = send_blocks[group][:, reader].astype(jnp.int32)
        received_in = init_blocks[group][owners, chosen]
        received_past = past_blocks[group][owners, chosen]
        output, grad_one, grad_two = reader_pass(tile_part, col_part, own_flat, received_in, received_past, weight_one, weight_two, cot_flat)
        return (carry[0] + grad_one, carry[1] + grad_two), output

    zeros = jnp.zeros((width, width), jnp.float32)
    indices = jnp.arange(N_GRP * N_DOM, dtype=jnp.int32)
    totals, outputs = lax.scan(step, (zeros, zeros), (tiles_all, cols_all, own_all, cot_all, indices))
    embeddings = outputs.reshape(N_GRP, N_DOM * NB * BS, width)
    return embeddings, totals[0], totals[1]
```

```python
import functools

import jax
import jax.numpy as jnp
from jax import lax
from jax.experimental import pallas as pl
from jax.experimental.pallas import tpu as pltpu
from jax.sharding import PartitionSpec as P

RESTART = 0.1
BETA_ONE = 0.405465
BETA_TWO = 0.223144

NZ = 8
NX = 4
NY = 4
STAGES = 4
MESH = pl.DeviceIdType.MESH


def dom_index(z, x, core):
    return (z * NX + x) * 2 + core


def exchange_kernel(
    initial_ref, history_ref, tiles_ref, meta_ref, out_ref,
    feat0, feat1, feat2, feat3, tiles_all, part_out, part_in, metas, metas_smem, table,
    z_recv, sib_recv, z_send, own_sem, t_recv, t_far, t_sib, t_send, t_own, p_recv, p_send,
    m_recv, m_send, m_copy,
):
    feats = (feat0, feat1, feat2, feat3)
    blocks, size, _ = initial_ref.shape
    slots = tiles_ref.shape[1]
    wide = feat0.shape[2]
    dom = lax.axis_index("dom")
    core = lax.rem(dom, 2)
    my_x = lax.rem(dom // 2, NX)
    my_z = dom // (2 * NX)
    other = 1 - core

    def at(dz, dx, flip):
        z = lax.rem(my_z + dz, NZ)
        x = lax.rem(my_x + dx, NX)
        return {"dom": dom_index(z, x, other if flip else core)}

    row = [(0, dx, f) for dx in range(NX) for f in range(2) if (dx, f) != (0, 0)]
    column = [(dz, 0, f) for dz in range(1, NZ) for f in range(2)]
    barrier = pltpu.get_barrier_semaphore()
    for peer in row + column:
        pl.semaphore_signal(barrier, inc=1, device_id=at(*peer), device_id_type=MESH)
    pl.semaphore_wait(barrier, len(row) + len(column))

    def remote(src, dst, send_sem, recv_sem, peer):
        return pltpu.make_async_remote_copy(
            src_ref=src, dst_ref=dst, send_sem=send_sem, recv_sem=recv_sem,
            device_id=at(*peer), device_id_type=MESH,
        )

    def feat_slot(stage, dz, flip):
        return feats[stage].at[pl.ds((dz * 2 + flip) * blocks, blocks)]

    def own_columns(stage, flip):
        ref = (initial_ref, history_ref)[stage // 2]
        half = other if flip else core
        start = pl.multiple_of((half * 2 + stage % 2) * wide, wide)
        return ref.at[:, :, pl.ds(start, wide)]

    def start_stage(stage):
        for flip in range(2):
            for direction, dz in ((0, 1), (1, NZ - 1)):
                remote(
                    own_columns(stage, flip), feat_slot(stage, NZ - dz, flip),
                    z_send.at[stage], z_recv.at[stage, direction, flip], (dz, 0, flip),
                ).start()
        remote(
            own_columns(stage, 1), feat_slot(stage, 0, 1),
            z_send.at[stage], sib_recv.at[stage], (0, 0, 1),
        ).start()
        pltpu.make_async_copy(own_columns(stage, 0), feat_slot(stage, 0, 0), own_sem.at[stage]).start()

    def land(ref, sem):
        pltpu.make_async_copy(ref, ref, sem).wait()

    def ring_tick(stage, m):
        for direction, dz in ((0, 1), (1, NZ - 1)):
            hop = m // 2 + 1
            flip = m % 2 if hop < NZ // 2 else direction
            origin = (NZ - hop if direction == 0 else hop) % NZ
            slot = feat_slot(stage, origin, flip)
            land(slot, z_recv.at[stage, direction, m])
            if hop < NZ // 2 - 1 or (hop == NZ // 2 - 1 and flip == direction):
                later = m + 2 if hop < NZ // 2 - 1 else NZ - 2
                next_origin = (NZ - hop - 1 if direction == 0 else hop + 1) % NZ
                remote(
                    slot, feat_slot(stage, next_origin, flip),
                    z_send.at[stage], z_recv.at[stage, direction, later], (dz, 0, 0),
                ).start()

    ticks = NZ - 1

    def tile_slot(dx, flip, i):
        return tiles_all.at[dx * 2 + flip, i]

    def send_tiles(rows):
        for n in rows:
            for i, dx, sem in ((n, 1, 0), (blocks - 1 - n, NX - 1, 1)):
                remote(
                    tiles_ref.at[i], tile_slot(NX - dx, 0, i), t_send, t_recv.at[sem, i], (0, dx, 0)
                ).start()

    def share_tiles(dx, i):
        remote(
            tile_slot(dx, 0, i), tile_slot(dx, 1, i), t_send, t_sib.at[dx, i], (0, 0, 1)
        ).start()

    def pass_tiles(rows):
        for n in rows:
            for i, dx, sem in ((n, NX - 1, 0), (blocks - 1 - n, 1, 1)):
                land(tile_slot(dx, 0, i), t_recv.at[sem, i])
                if n < blocks // 2:
                    toward = 1 if sem == 0 else NX - 1
                    remote(
                        tile_slot(dx, 0, i), tile_slot(2, 0, i), t_send, t_far.at[i], (0, toward, 0)
                    ).start()
                share_tiles(dx, i)

    near = [(0, 0, 1)] + [p for p in row if p[1] != 0] + column
    for peer in near:
        dz, dx, f = peer
        if dz == 0:
            slot = ((NX - dx) % NX) * 2 + f
        else:
            slot = 2 * NX + (NZ - dz - 1) * 2 + f
        remote(meta_ref, metas.at[slot], m_send, m_recv, peer).start()
    start_stage(0)
    for i in range(blocks):
        remote(tiles_ref.at[i], tile_slot(0, 1, i), t_send, t_sib.at[0, i], (0, 0, 1)).start()
    send_tiles(range(blocks // 2))
    own_tiles = pltpu.make_async_copy(tiles_ref, tiles_all.at[0], t_own)
    own_tiles.start()
    for f in feats:
        f[2 * NZ * blocks] = jnp.zeros((size, wide), f.dtype)
    metas[0] = meta_ref[...]

    def build_table():
        land(metas.at[pl.ds(1, len(near))], m_recv)
        copy = pltpu.make_async_copy(metas, metas_smem, m_copy)
        copy.start()
        copy.wait()

        for reader in range(2 * NX):
            dx, f = reader // 2, reader % 2
            reader_index = dom_index(my_z, lax.rem(my_x + dx, NX), other if f else core)

            def entry(n, carry):
                col = metas_smem[reader, 0, n]
                owner = jnp.maximum(col - blocks, 0)
                valid = (col >= blocks) & ((owner // 2) % NX == my_x)
                dz = (owner // (2 * NX) - my_z + NZ) % NZ
                flip = (owner + core) % 2
                where = jnp.where(dz == 0, flip, 2 * NX + (dz - 1) * 2 + flip)
                block = metas_smem[where, 1, reader_index]
                slot = (dz * 2 + flip) * blocks + block
                table[reader * blocks * slots + n] = jnp.where(valid, slot, 2 * NZ * blocks)
                return carry

            lax.fori_loop(0, blocks * slots, entry, 0)

    def partial(stage, reader):
        feat = feats[stage]

        def one(i, carry):
            first = (reader * blocks + i) * slots
            left = jnp.concatenate([tiles_all[reader, i, k] for k in range(slots)], axis=1)
            right = jnp.concatenate([feat[table[first + k]] for k in range(slots)], axis=0)
            total = jnp.dot(left, right, preferred_element_type=jnp.float32)
            part_out[stage, reader, i] = total.astype(part_out.dtype)
            return carry

        lax.fori_loop(0, blocks, one, 0)
        if reader:
            dx, f = reader // 2, reader % 2
            remote(
                part_out.at[stage, reader], part_in.at[stage, ((NX - dx) % NX) * 2 + f],
                p_send.at[stage], p_recv.at[stage], (0, dx, f),
            ).start()

    def finish(stage):
        land(part_in.at[stage, pl.ds(1, 2 * NX - 1)], p_recv.at[stage])
        for flip in range(2):
            half = other if flip else core
            for i in range(blocks):
                total = (part_in if flip else part_out)[stage, flip, i].astype(jnp.float32)
                for dx in range(1, NX):
                    total += part_in[stage, dx * 2 + flip, i].astype(jnp.float32)
                out_ref[stage // 2, half * 2 + stage % 2, i] = total

    order = (0, 1, 2, 3, 6, 7, 4, 5)
    last_order = (4, 5, 2, 3, 6, 7, 0, 1)

    def stage_ready(stage):
        land(feat_slot(stage, 0, 1), sib_recv.at[stage])
        land(feat_slot(stage, 0, 0), own_sem.at[stage])

    for stage in range(STAGES):
        for m in range(ticks):
            ring_tick(stage, m)
            if m == 2 and stage + 1 < STAGES:
                start_stage(stage + 1)
            if stage == 0:
                if m == 1:
                    send_tiles(range(blocks // 2, blocks))
                if m == 2:
                    build_table()
                if m == 5:
                    pass_tiles(range(blocks // 2))
            else:
                if stage == 1 and m == 0:
                    own_tiles.wait()
                    for i in range(blocks):
                        land(tile_slot(0, 1, i), t_sib.at[0, i])
                if stage == 1 and m == 1:
                    pass_tiles(range(blocks // 2, blocks))
                if stage == 1 and m == 2:
                    for i in range(blocks):
                        land(tile_slot(1, 1, i), t_sib.at[1, i])
                        land(tile_slot(NX - 1, 1, i), t_sib.at[NX - 1, i])
                if stage == 1 and m == 5:
                    for i in range(blocks):
                        land(tile_slot(2, 0, i), t_far.at[i])
                        share_tiles(2, i)
                if stage == 1 and m == 6:
                    for i in range(blocks):
                        land(tile_slot(2, 1, i), t_sib.at[2, i])
                partial(stage - 1, order[m])
                if m == ticks - 1:
                    partial(stage - 1, order[m + 1])
        stage_ready(stage)
    last = STAGES - 1
    for reader in last_order:
        partial(last, reader)
    for stage in range(STAGES):
        finish(stage)

    for stage in range(STAGES):
        sent = 15 * blocks
        land(feats[stage].at[pl.ds(0, sent)], z_send.at[stage])
        land(part_out.at[stage, pl.ds(1, 2 * NX - 1)], p_send.at[stage])
    for _ in range(1):
        land(metas.at[pl.ds(1, len(near))], m_send)
    land(tiles_all.at[pl.ds(1, 2 * NX - 1)], t_send)


def exchange(initial, history, tiles, meta):
    blocks, size, width = initial.shape
    slots = tiles.shape[1]
    wide = width // 4
    vmem = pl.BlockSpec(memory_space=pltpu.VMEM)
    dma = pltpu.SemaphoreType.DMA
    metas = 2 * NX + 2 * (NZ - 1)
    return pl.pallas_call(
        exchange_kernel,
        out_shape=jax.ShapeDtypeStruct((2, 4, blocks, size, wide), jnp.float32),
        in_specs=[vmem] * 4,
        out_specs=vmem,
        scratch_shapes=[pltpu.VMEM((2 * NZ * blocks + 1, size, wide), jnp.bfloat16)] * STAGES
        + [
            pltpu.VMEM((2 * NX, blocks, slots, size, size), jnp.bfloat16),
            pltpu.VMEM((STAGES, 2 * NX, blocks, size, wide), jnp.bfloat16),
            pltpu.VMEM((STAGES, 2 * NX, blocks, size, wide), jnp.bfloat16),
            pltpu.VMEM((metas, 8, 128), jnp.int32),
            pltpu.SMEM((metas, 8, 128), jnp.int32),
            pltpu.SMEM((2 * NX * blocks * slots,), jnp.int32),
            dma((STAGES, 2, NZ - 1)),
            dma((STAGES,)),
            dma((STAGES,)),
            dma((STAGES,)),
            dma((2, blocks)),
            dma((blocks,)),
            dma((NX, blocks)),
            dma,
            dma,
            dma((STAGES,)),
            dma((STAGES,)),
            dma,
            dma,
            dma,
        ],
        compiler_params=pltpu.CompilerParams(
            collective_id=0, has_side_effects=True, vmem_limit_bytes=56 * 2**20
        ),
        cost_estimate=pl.CostEstimate(
            flops=5 * 10**9, bytes_accessed=8 * 2**20, transcendentals=0
        ),
        name="exchange",
    )(initial, history, tiles, meta)


def sigmoid(value):
    return 1.0 / (1.0 + jnp.exp(-value))


def dense_kernel(
    initial_ref, tiles_ref, cols_ref, remote_ref, one_ref, two_ref, cot_ref,
    out_ref, grads_ref, local_ref,
):
    blocks, slots, size, _ = tiles_ref.shape
    width = initial_ref.shape[1]
    wide = width // 4
    f32 = jnp.float32

    def dot(a, b, dims=((1,), (0,))):
        return lax.dot_general(a, b, (dims, ((), ())), preferred_element_type=f32)

    for i in range(blocks):
        sums = [jnp.zeros((size, size), f32) for _ in range(blocks)]
        for k in range(slots):
            tile = tiles_ref[i, k].astype(f32)
            for c in range(blocks):
                mask = jnp.where(cols_ref[i, k] == c, 1.0, 0.0).astype(f32)
                sums[c] += tile * mask
        for c in range(blocks):
            local_ref[pl.ds(i * size, size), pl.ds(c * size, size)] = sums[c].astype(jnp.bfloat16)

    def received(which):
        return jnp.concatenate(
            [remote_ref[which, q].reshape(blocks * size, wide) for q in range(4)], axis=1
        )

    own = initial_ref[...]
    own_float = own.astype(f32)
    local = local_ref[...]
    mixed_one = (
        (1.0 - RESTART) * (dot(local, own) + received(0)) + RESTART * own_float
    ).astype(jnp.bfloat16)
    pre_one = (1.0 - BETA_ONE) * mixed_one.astype(f32) + BETA_ONE * dot(mixed_one, one_ref[...])
    sig_one = sigmoid(pre_one)
    hidden = (pre_one * sig_one).astype(jnp.bfloat16)
    slope_one = sig_one * (1.0 + pre_one * (1.0 - sig_one))
    mixed_two = (
        (1.0 - RESTART) * (dot(local, hidden) + received(1)) + RESTART * own_float
    ).astype(jnp.bfloat16)
    pre_two = (1.0 - BETA_TWO) * mixed_two.astype(f32) + BETA_TWO * dot(mixed_two, two_ref[...])
    sig_two = sigmoid(pre_two)
    out_ref[...] = (pre_two * sig_two).astype(jnp.bfloat16)
    slope_two = sig_two * (1.0 + pre_two * (1.0 - sig_two))
    back_two = (cot_ref[...].astype(f32) * slope_two).astype(jnp.bfloat16)
    grad_two = dot(mixed_two, back_two, ((0,), (0,)))
    back_mixed = (
        (1.0 - BETA_TWO) * back_two.astype(f32)
        + BETA_TWO * dot(back_two, two_ref[...], ((1,), (1,)))
    ).astype(jnp.bfloat16)
    back_hidden = (1.0 - RESTART) * dot(local, back_mixed, ((0,), (0,)))
    back_one = (back_hidden * slope_one).astype(jnp.bfloat16)
    grad_one = dot(mixed_one, back_one, ((0,), (0,)))
    for q in range(4):
        for g, grad in ((0, grad_one), (1, grad_two)):
            grads_ref[g, q] = grad[:, q * wide : (q + 1) * wide].astype(jnp.bfloat16)


def dense(initial, tiles, cols, received, weight_one, weight_two, cotangent):
    rows, width = initial.shape
    vmem = pl.BlockSpec(memory_space=pltpu.VMEM)
    smem = pl.BlockSpec(memory_space=pltpu.SMEM)
    return pl.pallas_call(
        dense_kernel,
        out_shape=(
            jax.ShapeDtypeStruct((rows, width), jnp.bfloat16),
            jax.ShapeDtypeStruct((2, 4, width, width // 4), jnp.bfloat16),
        ),
        in_specs=[vmem, vmem, smem, vmem, vmem, vmem, vmem],
        out_specs=(vmem, vmem),
        scratch_shapes=[pltpu.VMEM((rows, rows), jnp.bfloat16)],
        compiler_params=pltpu.CompilerParams(vmem_limit_bytes=56 * 2**20),
        cost_estimate=pl.CostEstimate(
            flops=2 * 10**9, bytes_accessed=8 * 2**20, transcendentals=2**19
        ),
        name="dense",
    )(initial, tiles, cols, received, weight_one, weight_two, cotangent)


def reduce_kernel(
    grads_ref, out_ref, pair_in, pair_sum, x_in, x_sum, far_in, done,
    pair_send, pair_recv, x_send, x_recv, far_send, far_recv,
    done_send, done_recv, gx_send, gx_recv, back_send, back_recv,
):
    f32 = jnp.float32
    dom = lax.axis_index("dom")
    my_y = lax.axis_index("grp")
    core = lax.rem(dom, 2)
    my_x = lax.rem(dom // 2, NX)
    my_z = dom // (2 * NX)
    other = 1 - core
    units = grads_ref.shape[1]
    per_x = units // NX

    def across(dx):
        return (dom_index(my_z, lax.rem(my_x + dx, NX), core), my_y)

    def plane(dz, dy):
        return (dom_index(lax.rem(my_z + dz, NZ), my_x, core), lax.rem(my_y + dy, NY))

    pair = (dom_index(my_z, my_x, other), my_y)
    spread = [(dz, dy) for dz in range(NZ) for dy in range(NY) if dz or dy]

    barrier = pltpu.get_barrier_semaphore()
    peers = [pair] + [across(dx) for dx in range(1, NX)] + [plane(*p) for p in spread]
    for peer in peers:
        pl.semaphore_signal(barrier, inc=1, device_id=peer, device_id_type=MESH)
    pl.semaphore_wait(barrier, len(peers))

    def remote(src, dst, send_sem, recv_sem, peer):
        return pltpu.make_async_remote_copy(
            src_ref=src, dst_ref=dst, send_sem=send_sem, recv_sem=recv_sem,
            device_id=peer, device_id_type=MESH,
        )

    def land(ref, sem):
        pltpu.make_async_copy(ref, ref, sem).wait()

    remote(grads_ref.at[other], pair_in, pair_send, pair_recv, pair).start()
    land(pair_in, pair_recv)
    pair_sum[...] = (grads_ref[core].astype(f32) + pair_in[...].astype(f32)).astype(pair_sum.dtype)

    for dx in range(1, NX):
        quarter = lax.rem(my_x + dx, NX)
        remote(
            pair_sum.at[pl.ds(quarter * per_x, per_x)], x_in.at[NX - dx - 1],
            x_send, x_recv, across(dx),
        ).start()
    total = pair_sum[pl.ds(my_x * per_x, per_x)].astype(f32)
    land(x_in, x_recv)
    for n in range(NX - 1):
        total += x_in[n].astype(f32)
    x_sum[...] = total.astype(x_sum.dtype)

    mine = my_z * NY + my_y
    for n, (dz, dy) in enumerate(spread):
        theirs = lax.rem(my_z + dz, NZ) * NY + lax.rem(my_y + dy, NY)
        back = ((NZ - dz) % NZ) * NY + (NY - dy) % NY - 1
        remote(
            x_sum.at[theirs], far_in.at[back], far_send, far_recv, plane(dz, dy)
        ).start()
    land(far_in, far_recv)
    unit = x_sum[mine].astype(f32)
    for n in range(len(spread)):
        unit += far_in[n].astype(f32)
    done[mine] = unit.astype(done.dtype)

    for n, (dz, dy) in enumerate(spread):
        remote(
            done.at[mine], done.at[mine], done_send, done_recv, plane(dz, dy)
        ).start()
    land(done.at[pl.ds(0, len(spread))], done_recv)
    here = pl.ds(my_x * per_x, per_x)
    for dx in range(1, NX):
        remote(done, out_ref.at[core, here], gx_send, gx_recv.at[NX - dx - 1], across(dx)).start()
    remote(done, out_ref.at[core, here], back_send, back_recv.at[0], pair).start()
    out_ref[core, here] = done[...]
    for dx in (1, NX - 1, 2):
        got = pl.ds(lax.rem(my_x + dx, NX) * per_x, per_x)
        land(out_ref.at[core, got], gx_recv.at[dx - 1])
        remote(
            out_ref.at[core, got], out_ref.at[core, got], back_send, back_recv.at[dx], pair
        ).start()
    for dx in range(NX):
        got = pl.ds(lax.rem(my_x + dx, NX) * per_x, per_x)
        land(out_ref.at[other, got], back_recv.at[dx])

    land(pair_in, pair_send)
    land(x_in, x_send)
    land(far_in, far_send)
    land(far_in, done_send)
    land(x_in, gx_send)
    land(pair_in, back_send)


def reduce_all(grads):
    _, units, rows, lanes = grads.shape
    per_x = units // NX
    vmem = pl.BlockSpec(memory_space=pltpu.VMEM)
    dma = pltpu.SemaphoreType.DMA
    bf16 = grads.dtype
    return pl.pallas_call(
        reduce_kernel,
        out_shape=jax.ShapeDtypeStruct(grads.shape, bf16),
        in_specs=[vmem],
        out_specs=vmem,
        scratch_shapes=[
            pltpu.VMEM((units, rows, lanes), bf16),
            pltpu.VMEM((units, rows, lanes), bf16),
            pltpu.VMEM((NX - 1, per_x, rows, lanes), bf16),
            pltpu.VMEM((per_x, rows, lanes), bf16),
            pltpu.VMEM((NZ * NY - 1, rows, lanes), bf16),
            pltpu.VMEM((per_x, rows, lanes), bf16),
            dma, dma, dma, dma, dma, dma, dma, dma,
            dma,
            dma((NX - 1,)),
            dma,
            dma((NX,)),
        ],
        compiler_params=pltpu.CompilerParams(
            collective_id=1, has_side_effects=True, vmem_limit_bytes=32 * 2**20
        ),
        cost_estimate=pl.CostEstimate(flops=10**6, bytes_accessed=2 * 2**20, transcendentals=0),
        name="reduce_all",
    )(grads)


def local(initial, history, tile_values, tile_cols, send_blocks, weight_one, weight_two, cotangent):
    tiles = tile_values[0]
    cols = tile_cols[0]
    blocks, slots, size, _ = tiles.shape
    width = initial.shape[2]
    meta = jnp.concatenate(
        [
            jnp.pad(cols.reshape(1, blocks * slots), ((0, 0), (0, 128 - blocks * slots))),
            jnp.pad(send_blocks[0], ((0, 0), (0, 128 - send_blocks.shape[2]))),
            jnp.zeros((6, 128), jnp.int32),
        ],
        axis=0,
    )
    received = exchange(
        initial[0].reshape(blocks, size, width), history[0].reshape(blocks, size, width), tiles, meta
    )
    output, grads = dense(initial[0], tiles, cols, received, weight_one, weight_two, cotangent[0])
    wide = width // 4
    summed = reduce_all(grads.reshape(2, 4 * width // 16, 16, wide))
    summed = summed.reshape(2, 4, width, wide).transpose(0, 2, 1, 3).reshape(2, width, width)
    grad_one = BETA_ONE * summed[0].astype(jnp.float32)
    grad_two = BETA_TWO * summed[1].astype(jnp.float32)
    return (output[None], grad_one, grad_two)


def solution(mesh):
    return jax.shard_map(
        local,
        mesh=mesh,
        in_specs=(
            P("grp", "dom", None),
            P("grp", "dom", None),
            P("grp", "dom", None, None, None),
            P("grp", "dom", None),
            P("grp", "dom", None),
            P(),
            P(),
            P("grp", "dom", None),
        ),
        out_specs=(P("grp", "dom", None), P(), P()),
        check_vma=False,
    )
```

```python
import functools

import jax
import jax.numpy as jnp
from jax import lax
from jax.experimental import pallas as pl
from jax.experimental.pallas import tpu as pltpu
from jax.sharding import PartitionSpec as P

RESTART = 0.1
BETA_ONE = 0.405465
BETA_TWO = 0.223144

NZ = 8
NX = 4
NY = 4
STAGES = 4
MESH = pl.DeviceIdType.MESH


def dom_index(z, x, core):
    return (z * NX + x) * 2 + core


def sigmoid(value):
    return 1.0 / (1.0 + jnp.exp(-value))


def dot(a, b, dims=((1,), (0,))):
    return lax.dot_general(a, b, (dims, ((), ())), preferred_element_type=jnp.float32)


def layers_kernel(
    initial_ref, history_ref, tiles_ref, cols_ref, chosen_ref, one_ref, two_ref, cot_ref,
    out_ref, sum_ref,
    feat0, feat1, feat2, feat3, tiles_all, part_out, part_in, relay_in, metas, metas_smem, table,
    local_ref, base_ref, received_ref, mixed_one_ref, mixed_two_ref, hidden_ref, slope_ref,
    grad_ref, send_ref, pair_in, pair_sum, first_in, first_sum, first_out, second_in,
    third, third_in, third_done,
    z_recv, sib_recv, z_send, own_sem, t_recv, t_far, t_sib, t_send, t_own, p_recv, p_send,
    relay_recv, relay_send, m_recv, m_send, m_copy, pair_sems, first_send, first_recv,
    second_send, second_recv, third_send, third_recv, done_send, done_recv,
    gather_send, gather_recv, share_send, share_recv, back_send, back_recv,
):
    f32 = jnp.float32
    bf16 = jnp.bfloat16
    feats = (feat0, feat1, feat2, feat3)
    blocks, size, width = initial_ref.shape
    slots = tiles_ref.shape[1]
    wide = feat0.shape[2]
    rows = blocks * size
    dom = lax.axis_index("dom")
    my_y = lax.axis_index("grp")
    core = lax.rem(dom, 2)
    my_x = lax.rem(dom // 2, NX)
    my_z = dom // (2 * NX)
    other = 1 - core

    def at(dz, dx, flip, dy=0):
        z = lax.rem(my_z + dz, NZ)
        x = lax.rem(my_x + dx, NX)
        y = lax.rem(my_y + dy, NY)
        return (dom_index(z, x, other if flip else core), y)

    row = [(0, dx, f) for dx in range(NX) for f in range(2) if (dx, f) != (0, 0)]
    column = [(dz, 0, f) for dz in range(1, NZ) for f in range(2)]
    stack = [(0, 0, 0, dy) for dy in range(1, NY)]
    barrier = pltpu.get_barrier_semaphore()
    for peer in row + column + stack:
        pl.semaphore_signal(barrier, inc=1, device_id=at(*peer), device_id_type=MESH)
    pl.semaphore_wait(barrier, len(row) + len(column) + len(stack))

    def remote(src, dst, send_sem, recv_sem, peer):
        return pltpu.make_async_remote_copy(
            src_ref=src, dst_ref=dst, send_sem=send_sem, recv_sem=recv_sem,
            device_id=at(*peer), device_id_type=MESH,
        )

    def land(ref, sem):
        pltpu.make_async_copy(ref, ref, sem).wait()

    def feat_slot(stage, dz, flip):
        return feats[stage].at[pl.ds((dz * 2 + flip) * blocks, blocks)]

    def own_columns(stage, flip):
        ref = (initial_ref, history_ref)[stage // 2]
        half = other if flip else core
        start = pl.multiple_of((half * 2 + stage % 2) * wide, wide)
        return ref.at[:, :, pl.ds(start, wide)]

    def start_stage(stage):
        for flip in range(2):
            for direction, dz in ((0, 1), (1, NZ - 1)):
                remote(
                    own_columns(stage, flip), feat_slot(stage, NZ - dz, flip),
                    z_send.at[stage], z_recv.at[stage, direction, flip], (dz, 0, flip),
                ).start()
        remote(
            own_columns(stage, 1), feat_slot(stage, 0, 1),
            z_send.at[stage], sib_recv.at[stage], (0, 0, 1),
        ).start()
        pltpu.make_async_copy(own_columns(stage, 0), feat_slot(stage, 0, 0), own_sem.at[stage]).start()

    def ring_tick(stage, m):
        for direction, dz in ((0, 1), (1, NZ - 1)):
            hop = m // 2 + 1
            flip = m % 2 if hop < NZ // 2 else direction
            origin = (NZ - hop if direction == 0 else hop) % NZ
            slot = feat_slot(stage, origin, flip)
            land(slot, z_recv.at[stage, direction, m])
            if hop < NZ // 2 - 1 or (hop == NZ // 2 - 1 and flip == direction):
                later = m + 2 if hop < NZ // 2 - 1 else NZ - 2
                next_origin = (NZ - hop - 1 if direction == 0 else hop + 1) % NZ
                remote(
                    slot, feat_slot(stage, next_origin, flip),
                    z_send.at[stage], z_recv.at[stage, direction, later], (dz, 0, 0),
                ).start()

    def tile_slot(dx, flip, i):
        return tiles_all.at[dx * 2 + flip, i]

    def send_tiles(which):
        for n in which:
            for i, dx, sem in ((n, 1, 0), (blocks - 1 - n, NX - 1, 1)):
                remote(
                    tiles_ref.at[i], tile_slot(NX - dx, 0, i), t_send, t_recv.at[sem, i], (0, dx, 0)
                ).start()

    def share_tiles(dx, i):
        remote(
            tile_slot(dx, 0, i), tile_slot(dx, 1, i), t_send, t_sib.at[dx, i], (0, 0, 1)
        ).start()

    def pass_tiles(which):
        for n in which:
            for i, dx, sem in ((n, NX - 1, 0), (blocks - 1 - n, 1, 1)):
                land(tile_slot(dx, 0, i), t_recv.at[sem, i])
                if n < blocks // 2:
                    toward = 1 if sem == 0 else NX - 1
                    remote(
                        tile_slot(dx, 0, i), tile_slot(2, 0, i), t_send, t_far.at[i], (0, toward, 0)
                    ).start()
                share_tiles(dx, i)

    near = [(0, 0, 1)] + [p for p in row if p[1] != 0] + column
    metas[0, pl.ds(0, blocks), pl.ds(0, slots)] = cols_ref[...]
    metas[0, pl.ds(blocks, 1), pl.ds(0, chosen_ref.shape[1])] = chosen_ref[...]
    start_stage(0)
    for peer in near:
        dz, dx, f = peer
        if dz == 0:
            slot = ((NX - dx) % NX) * 2 + f
        else:
            slot = 2 * NX + (NZ - dz - 1) * 2 + f
        remote(metas.at[0], metas.at[slot], m_send, m_recv, peer).start()
    for i in range(blocks):
        remote(tiles_ref.at[i], tile_slot(0, 1, i), t_send, t_sib.at[0, i], (0, 0, 1)).start()
    send_tiles(range(blocks // 2))
    own_tiles = pltpu.make_async_copy(tiles_ref, tiles_all.at[0], t_own)
    own_tiles.start()
    for f in feats:
        f[2 * NZ * blocks] = jnp.zeros((size, wide), f.dtype)

    def copy_metas():
        land(metas.at[pl.ds(1, len(near))], m_recv)
        copy = pltpu.make_async_copy(metas, metas_smem, m_copy)
        copy.start()
        copy.wait()

    def build_table(readers):
        for reader in readers:
            dx, f = reader // 2, reader % 2
            reader_index = dom_index(my_z, lax.rem(my_x + dx, NX), other if f else core)

            def entry(n, carry):
                col = metas_smem[reader, n // slots, n % slots]
                owner = jnp.maximum(col - blocks, 0)
                valid = (col >= blocks) & ((owner // 2) % NX == my_x)
                dz = (owner // (2 * NX) - my_z + NZ) % NZ
                flip = (owner + core) % 2
                where = jnp.where(dz == 0, flip, 2 * NX + (dz - 1) * 2 + flip)
                block = metas_smem[where, blocks, reader_index]
                slot = (dz * 2 + flip) * blocks + block
                table[reader * blocks * slots + n] = jnp.where(valid, slot, 2 * NZ * blocks)
                return carry

            lax.fori_loop(0, blocks * slots, entry, 0)

    def build_local(i):
        sums = [jnp.zeros((size, size), f32) for _ in range(blocks)]
        for k in range(slots):
            tile = tiles_ref[i, k].astype(f32)
            for c in range(blocks):
                mask = jnp.where(metas_smem[0, i, k] == c, 1.0, 0.0).astype(f32)
                sums[c] += tile * mask
        for c in range(blocks):
            local_ref[pl.ds(i * size, size), pl.ds(c * size, size)] = sums[c].astype(bf16)

    def partial(stage, reader):
        feat = feats[stage]
        last = stage == STAGES - 1
        dx, f = reader // 2, reader % 2
        relays = (dx, f) in ((1, 0), (NX - 1, 1))
        if relays and not last:
            land(relay_in.at[stage, f], relay_recv.at[stage, f, 0])

        def send(which):
            if dx == 2:
                toward = 1 if f == 0 else NX - 1
                remote(
                    part_out.at[stage, reader, which], relay_in.at[stage, f, which],
                    relay_send.at[stage], relay_recv.at[stage, f, which if last else 0],
                    (0, toward, 0),
                ).start()
            elif reader:
                source = {0: 0, 1: 2, NX - 1: 1}[dx]
                remote(
                    part_out.at[stage, reader, which], part_in.at[stage, source * 2 + f, which],
                    p_send.at[stage], p_recv.at[stage], (0, dx, f),
                ).start()

        def one(i, carry):
            first = (reader * blocks + i) * slots
            left = jnp.concatenate([tiles_all[reader, i, k] for k in range(slots)], axis=1)
            right = jnp.concatenate([feat[table[first + k]] for k in range(slots)], axis=0)
            total = dot(left, right)
            if relays:
                if last:
                    land(relay_in.at[stage, f, i], relay_recv.at[stage, f, i])
                total += relay_in[stage, f, i].astype(f32)
            part_out[stage, reader, i] = total.astype(bf16)
            if last:
                send(i)
            return carry

        if last:
            for i in range(blocks):
                one(i, 0)
        else:
            lax.fori_loop(0, blocks, one, 0)
            send(slice(None))

    def column_chunk(stage, flip):
        return (other if flip else core) * 2 + stage % 2

    def total_of(stage, flip):
        first = part_in[stage, 1] if flip else part_out[stage, 0]
        total = first.astype(f32)
        for source in (1, 2):
            total += part_in[stage, source * 2 + flip].astype(f32)
        return total.reshape(rows, wide)

    def received(stage):
        land(part_in.at[stage, pl.ds(1, 5)], p_recv.at[stage])

    def finish_one(stage):
        received(stage)
        for flip in range(2):
            received_ref[column_chunk(stage, flip)] = total_of(stage, flip)

    def layer_one(i):
        here = pl.ds(i * size, size)
        local = local_ref[here, :]
        own = initial_ref[...].reshape(rows, width)
        got = jnp.concatenate([received_ref[q, here, :] for q in range(4)], axis=1)
        mixed = (
            (1.0 - RESTART) * (dot(local, own) + got) + RESTART * initial_ref[i].astype(f32)
        ).astype(bf16)
        pre = (1.0 - BETA_ONE) * mixed.astype(f32) + BETA_ONE * dot(mixed, one_ref[...])
        sig = sigmoid(pre)
        mixed_one_ref[here, :] = mixed
        hidden_ref[here, :] = (pre * sig).astype(bf16)
        slope_ref[here, :] = sig * (1.0 + pre * (1.0 - sig))

    def start_two():
        total = (1.0 - RESTART) * dot(local_ref[...], hidden_ref[...]) + RESTART * initial_ref[
            ...
        ].reshape(rows, width).astype(f32)
        for q in range(4):
            base_ref[q] = total[:, q * wide : (q + 1) * wide]

    def finish_two(stage):
        received(stage)
        for flip in range(2):
            chunk = column_chunk(stage, flip)
            mixed = base_ref[chunk] + (1.0 - RESTART) * total_of(stage, flip)
            mixed_two_ref[:, pl.ds(pl.multiple_of(chunk * wide, wide), wide)] = mixed.astype(bf16)

    def store_grad(g, grad):
        grad_ref[g] = grad
        send_ref[g] = grad.astype(bf16)

    def layer_two():
        mixed_two = mixed_two_ref[...]
        pre_two = (1.0 - BETA_TWO) * mixed_two.astype(f32) + BETA_TWO * dot(mixed_two, two_ref[...])
        sig = sigmoid(pre_two)
        out_ref[...] = (pre_two * sig).astype(bf16)
        slope_two = sig * (1.0 + pre_two * (1.0 - sig))
        back_two = (cot_ref[...].astype(f32) * slope_two).astype(bf16)
        back_mixed = (
            (1.0 - BETA_TWO) * back_two.astype(f32)
            + BETA_TWO * dot(back_two, two_ref[...], ((1,), (1,)))
        ).astype(bf16)
        back_hidden = (1.0 - RESTART) * dot(local_ref[...], back_mixed, ((0,), (0,)))
        back_one = (back_hidden * slope_ref[...]).astype(bf16)
        store_grad(1, dot(mixed_two, back_two, ((0,), (0,))))
        store_grad(0, dot(mixed_one_ref[...], back_one, ((0,), (0,))))

    order = [(2, 0), (2, 1), (1, 1), (3, 0), (1, 0), (3, 1), (0, 1), (0, 0)]
    first_order = [(0, 1), (0, 0), (1, 1), (3, 0), (2, 0), (2, 1), (1, 0), (3, 1)]

    for stage in range(STAGES):
        for m in range(NZ - 1):
            ring_tick(stage, m)
            if m == 2 and stage + 1 < STAGES:
                start_stage(stage + 1)
            if stage == 0:
                if m == 1:
                    send_tiles(range(blocks // 2, blocks))
                    copy_metas()
                if m >= 2 and m < 6:
                    build_table((2 * (m - 2), 2 * (m - 2) + 1))
                    build_local(m - 2)
                if m == 5:
                    pass_tiles(range(blocks // 2))
                continue
            if stage == 1:
                if m == 0:
                    own_tiles.wait()
                    for i in range(blocks):
                        land(tile_slot(0, 1, i), t_sib.at[0, i])
                if m == 1:
                    pass_tiles(range(blocks // 2, blocks))
                if m == 2:
                    for i in range(blocks):
                        land(tile_slot(1, 1, i), t_sib.at[1, i])
                        land(tile_slot(NX - 1, 1, i), t_sib.at[NX - 1, i])
                if m == 4:
                    for i in range(blocks):
                        land(tile_slot(2, 0, i), t_far.at[i])
                        share_tiles(2, i)
                if m == 5:
                    for i in range(blocks):
                        land(tile_slot(2, 1, i), t_sib.at[2, i])
            turns = [m] if m < NZ - 2 else [m, m + 1]
            for turn in turns:
                dx, f = (first_order if stage == 1 else order)[turn]
                partial(stage - 1, dx * 2 + f)
            if stage == STAGES - 1:
                if m == 0:
                    finish_one(0)
                if m == 2:
                    finish_one(1)
                if m >= 3:
                    layer_one(m - 3)
        land(feat_slot(stage, 0, 1), sib_recv.at[stage])
        land(feat_slot(stage, 0, 0), own_sem.at[stage])
    for dx, f in order:
        partial(STAGES - 1, dx * 2 + f)
    start_two()
    finish_two(2)
    finish_two(3)
    layer_two()

    remote(send_ref.at[other], pair_in, pair_sems.at[0], pair_sems.at[1], (0, 0, 1)).start()
    land(pair_in, pair_sems.at[1])
    pair_sum[...] = (grad_ref[core] + pair_in[...].astype(f32)).astype(bf16)

    half = width // 2
    quarter = half // NX
    part = quarter // NX
    place = ((my_x, my_y), (my_y, my_x))

    def rows_at(start, count):
        return pl.ds(pl.multiple_of(start, part), count)

    def along(h, turn, d):
        return (0, d, 0) if h == turn else (0, 0, 0, d)

    for d in (2, 1, 3):
        for h in range(2):
            theirs = rows_at(h * half + lax.rem(place[h][0] + d, NX) * quarter, quarter)
            remote(
                pair_sum.at[theirs], first_in.at[h, NX - d - 1],
                first_send, first_recv.at[h], along(h, 0, d),
            ).start()
    for h in range(2):
        mine = rows_at(h * half + place[h][0] * quarter, quarter)
        value = grad_ref[core, mine, :] + pair_in[mine, :].astype(f32)
        land(first_in.at[h], first_recv.at[h])
        for n in range(NX - 1):
            value += first_in[h, n].astype(f32)
        first_sum[h] = value
        first_out[h] = value.astype(bf16)
        for d in (2, 1, 3):
            theirs = rows_at(lax.rem(place[h][1] + d, NX) * part, part)
            remote(
                first_out.at[h, theirs], second_in.at[h, NX - d - 1],
                second_send, second_recv.at[h], along(h, 1, d),
            ).start()
    tiles_of = [(r, q) for r in range(part // 8) for q in range(4)]
    for h in range(2):
        value = first_sum[h, rows_at(place[h][1] * part, part), :]
        land(second_in.at[h], second_recv.at[h])
        for n in range(NX - 1):
            value += second_in[h, n].astype(f32)
        for n, (r, q) in enumerate(tiles_of):
            third[h, n] = value[r * 8 : (r + 1) * 8, q * wide : (q + 1) * wide]
        for dz in range(1, NZ):
            remote(
                third.at[h, lax.rem(my_z + dz, NZ)], third_in.at[h, NZ - dz - 1],
                third_send, third_recv.at[h], (dz, 0, 0),
            ).start()
    for h in range(2):
        value = third[h, my_z]
        land(third_in.at[h], third_recv.at[h])
        for n in range(NZ - 1):
            value += third_in[h, n]
        third_done[h, my_z] = value
        for dz in range(1, NZ):
            remote(
                third_done.at[h, my_z], third_done.at[h, my_z],
                done_send, done_recv.at[h], (dz, 0, 0),
            ).start()

    for h in range(2):
        land(third_done.at[h, pl.ds(0, NZ - 1)], done_recv.at[h])
        value = jnp.concatenate(
            [
                jnp.concatenate([third_done[h, r * 4 + q] for q in range(4)], axis=1)
                for r in range(part // 8)
            ],
            axis=0,
        )
        mine = rows_at(h * half + place[h][0] * quarter + place[h][1] * part, part)
        sum_ref[core, mine, :] = value.astype(bf16)
        for d in (2, 1, 3):
            remote(
                sum_ref.at[core, mine], sum_ref.at[core, mine],
                gather_send, gather_recv.at[h], along(h, 1, d),
            ).start()
    for h in range(2):
        land(second_in.at[h], gather_recv.at[h])
        mine = rows_at(h * half + place[h][0] * quarter, quarter)
        for d in (2, 1, 3):
            remote(
                sum_ref.at[core, mine], sum_ref.at[core, mine],
                share_send, share_recv.at[h, NX - d - 1], along(h, 0, d),
            ).start()
        remote(
            sum_ref.at[core, mine], sum_ref.at[core, mine],
            back_send, back_recv.at[h, 0], (0, 0, 1),
        ).start()

    def share_at(h, d):
        return rows_at(h * half + lax.rem(place[h][0] + d, NX) * quarter, quarter)

    for d in (1, 3, 2):
        for h in range(2):
            got = share_at(h, d)
            land(sum_ref.at[core, got], share_recv.at[h, d - 1])
            remote(
                sum_ref.at[core, got], sum_ref.at[core, got],
                back_send, back_recv.at[h, d], (0, 0, 1),
            ).start()
    for d in range(NX):
        for h in range(2):
            land(sum_ref.at[other, share_at(h, d)], back_recv.at[h, d])

    for stage in range(STAGES):
        land(feats[stage].at[pl.ds(0, 15 * blocks)], z_send.at[stage])
        land(part_in.at[stage, pl.ds(1, 5)], p_send.at[stage])
        land(relay_in.at[stage], relay_send.at[stage])
    land(metas.at[pl.ds(1, len(near))], m_send)
    land(tiles_all.at[pl.ds(1, 2 * NX - 1)], t_send)
    land(pair_in, pair_sems.at[0])
    land(first_in, first_send)
    land(second_in, second_send)
    land(third_in, third_send)
    land(third_in, done_send)
    land(second_in, gather_send)
    land(first_in, share_send)
    land(pair_in, back_send)


def layers(initial, history, tiles, cols, chosen, weight_one, weight_two, cotangent):
    blocks, size, width = initial.shape
    slots = tiles.shape[1]
    wide = width // 4
    rows = blocks * size
    quarter = width // 2 // NX
    part = quarter // NX
    vmem = pl.BlockSpec(memory_space=pltpu.VMEM)
    dma = pltpu.SemaphoreType.DMA
    bf16 = jnp.bfloat16
    f32 = jnp.float32
    metas = 2 * NX + 2 * (NZ - 1)
    return pl.pallas_call(
        layers_kernel,
        out_shape=(
            jax.ShapeDtypeStruct((rows, width), bf16),
            jax.ShapeDtypeStruct((2, width, width), bf16),
        ),
        in_specs=[vmem] * 8,
        out_specs=(vmem, vmem),
        scratch_shapes=[pltpu.VMEM((2 * NZ * blocks + 1, size, wide), bf16)] * STAGES
        + [
            pltpu.VMEM((2 * NX, blocks, slots, size, size), bf16),
            pltpu.VMEM((STAGES, 2 * NX, blocks, size, wide), bf16),
            pltpu.VMEM((STAGES, 6, blocks, size, wide), bf16),
            pltpu.VMEM((STAGES, 2, blocks, size, wide), bf16),
            pltpu.VMEM((metas, 8, 128), jnp.int32),
            pltpu.SMEM((metas, 8, 128), jnp.int32),
            pltpu.SMEM((2 * NX * blocks * slots,), jnp.int32),
            pltpu.VMEM((rows, rows), bf16),
            pltpu.VMEM((4, rows, wide), f32),
            pltpu.VMEM((4, rows, wide), f32),
            pltpu.VMEM((rows, width), bf16),
            pltpu.VMEM((rows, width), bf16),
            pltpu.VMEM((rows, width), bf16),
            pltpu.VMEM((rows, width), f32),
            pltpu.VMEM((2, width, width), f32),
            pltpu.VMEM((2, width, width), bf16),
            pltpu.VMEM((width, width), bf16),
            pltpu.VMEM((width, width), bf16),
            pltpu.VMEM((2, NX - 1, quarter, width), bf16),
            pltpu.VMEM((2, quarter, width), f32),
            pltpu.VMEM((2, quarter, width), bf16),
            pltpu.VMEM((2, NX - 1, part, width), bf16),
            pltpu.VMEM((2, NZ, 8, wide), f32),
            pltpu.VMEM((2, NZ - 1, 8, wide), f32),
            pltpu.VMEM((2, NZ, 8, wide), f32),
            dma((STAGES, 2, NZ - 1)),
            dma((STAGES,)),
            dma((STAGES,)),
            dma((STAGES,)),
            dma((2, blocks)),
            dma((blocks,)),
            dma((NX, blocks)),
            dma,
            dma,
            dma((STAGES,)),
            dma((STAGES,)),
            dma((STAGES, 2, blocks)),
            dma((STAGES,)),
            dma,
            dma,
            dma,
            dma((2,)),
            dma,
            dma((2,)),
            dma,
            dma((2,)),
            dma,
            dma((2,)),
            dma,
            dma((2,)),
            dma,
            dma((2,)),
            dma,
            dma((2, NX - 1)),
            dma,
            dma((2, NX)),
        ],
        compiler_params=pltpu.CompilerParams(
            collective_id=0, has_side_effects=True, vmem_limit_bytes=56 * 2**20
        ),
        cost_estimate=pl.CostEstimate(
            flops=7 * 10**9, bytes_accessed=8 * 2**20, transcendentals=2**19
        ),
        name="layers",
    )(initial, history, tiles, cols, chosen, weight_one, weight_two, cotangent)


def local(initial, history, tile_values, tile_cols, send_blocks, weight_one, weight_two, cotangent):
    tiles = tile_values[0]
    blocks, slots, size, _ = tiles.shape
    width = initial.shape[2]
    output, summed = layers(
        initial[0].reshape(blocks, size, width), history[0].reshape(blocks, size, width),
        tiles, tile_cols[0], send_blocks[0], weight_one, weight_two, cotangent[0],
    )
    grad_one = BETA_ONE * summed[0].astype(jnp.float32)
    grad_two = BETA_TWO * summed[1].astype(jnp.float32)
    return (output[None], grad_one, grad_two)


def solution(mesh):
    return jax.shard_map(
        local,
        mesh=mesh,
        in_specs=(
            P("grp", "dom", None),
            P("grp", "dom", None),
            P("grp", "dom", None, None, None),
            P("grp", "dom", None),
            P("grp", "dom", None),
            P(),
            P(),
            P("grp", "dom", None),
        ),
        out_specs=(P("grp", "dom", None), P(), P()),
        check_vma=False,
    )
```

```python
import functools

import jax
import jax.numpy as jnp
from jax import lax
from jax.experimental import pallas as pl
from jax.experimental.pallas import tpu as pltpu
from jax.sharding import PartitionSpec as P

RESTART = 0.1
BETA_ONE = 0.405465
BETA_TWO = 0.223144

NZ = 8
NX = 4
NY = 4
STAGES = 4
MESH = pl.DeviceIdType.MESH


def dom_index(z, x, core):
    return (z * NX + x) * 2 + core


def sigmoid(value):
    return 1.0 / (1.0 + jnp.exp(-value))


def dot(a, b, dims=((1,), (0,))):
    return lax.dot_general(a, b, (dims, ((), ())), preferred_element_type=jnp.float32)


def layers_kernel(
    initial_ref, history_ref, tiles_ref, cols_ref, chosen_ref, one_ref, two_ref, cot_ref,
    out_ref, sum_ref,
    feat0, feat1, feat2, feat3, tiles_all, part_out, part_in, relay_in, relay_sum, metas, metas_smem, table,
    local_ref, base_ref, received_ref, mixed_one_ref, mixed_two_ref, hidden_ref, slope_ref,
    grad_ref, send_ref, pair_in, pair_sum, first_in, first_sum, first_out, second_in,
    third, third_in, third_done,
    z_recv, sib_recv, z_send, own_sem, t_recv, t_far, t_sib, t_send, t_own, p_recv, p_send,
    relay_recv, relay_send, m_recv, m_send, m_copy, pair_sems, first_send, first_recv,
    second_send, second_recv, third_send, third_recv, done_send, done_recv,
    gather_send, gather_recv, share_send, share_recv, back_send, back_recv,
):
    f32 = jnp.float32
    bf16 = jnp.bfloat16
    feats = (feat0, feat1, feat2, feat3)
    blocks, size, width = initial_ref.shape
    slots = tiles_ref.shape[1]
    wide = feat0.shape[2]
    rows = blocks * size
    dom = lax.axis_index("dom")
    my_y = lax.axis_index("grp")
    core = lax.rem(dom, 2)
    my_x = lax.rem(dom // 2, NX)
    my_z = dom // (2 * NX)
    other = 1 - core

    def at(dz, dx, flip, dy=0):
        z = lax.rem(my_z + dz, NZ)
        x = lax.rem(my_x + dx, NX)
        y = lax.rem(my_y + dy, NY)
        return (dom_index(z, x, other if flip else core), y)

    row = [(0, dx, f) for dx in range(NX) for f in range(2) if (dx, f) != (0, 0)]
    column = [(dz, 0, f) for dz in range(1, NZ) for f in range(2)]
    stack = [(0, 0, 0, dy) for dy in range(1, NY)]
    barrier = pltpu.get_barrier_semaphore()
    for peer in row + column + stack:
        pl.semaphore_signal(barrier, inc=1, device_id=at(*peer), device_id_type=MESH)
    pl.semaphore_wait(barrier, len(row) + len(column) + len(stack))

    def remote(src, dst, send_sem, recv_sem, peer):
        return pltpu.make_async_remote_copy(
            src_ref=src, dst_ref=dst, send_sem=send_sem, recv_sem=recv_sem,
            device_id=at(*peer), device_id_type=MESH,
        )

    def land(ref, sem):
        pltpu.make_async_copy(ref, ref, sem).wait()

    def feat_slot(stage, dz, flip):
        return feats[stage].at[pl.ds((dz * 2 + flip) * blocks, blocks)]

    def own_columns(stage, flip):
        ref = (initial_ref, history_ref)[stage // 2]
        half = other if flip else core
        start = pl.multiple_of((half * 2 + stage % 2) * wide, wide)
        return ref.at[:, :, pl.ds(start, wide)]

    def start_stage(stage):
        for flip in range(2):
            for direction, dz in ((0, 1), (1, NZ - 1)):
                remote(
                    own_columns(stage, flip), feat_slot(stage, NZ - dz, flip),
                    z_send.at[stage], z_recv.at[stage, direction, flip], (dz, 0, flip),
                ).start()
        remote(
            own_columns(stage, 1), feat_slot(stage, 0, 1),
            z_send.at[stage], sib_recv.at[stage], (0, 0, 1),
        ).start()
        pltpu.make_async_copy(own_columns(stage, 0), feat_slot(stage, 0, 0), own_sem.at[stage]).start()

    def ring_tick(stage, m):
        for direction, dz in ((0, 1), (1, NZ - 1)):
            hop = m // 2 + 1
            flip = m % 2 if hop < NZ // 2 else direction
            origin = (NZ - hop if direction == 0 else hop) % NZ
            slot = feat_slot(stage, origin, flip)
            land(slot, z_recv.at[stage, direction, m])
            if hop < NZ // 2 - 1 or (hop == NZ // 2 - 1 and flip == direction):
                later = m + 2 if hop < NZ // 2 - 1 else NZ - 2
                next_origin = (NZ - hop - 1 if direction == 0 else hop + 1) % NZ
                remote(
                    slot, feat_slot(stage, next_origin, flip),
                    z_send.at[stage], z_recv.at[stage, direction, later], (dz, 0, 0),
                ).start()

    def tile_slot(dx, flip, i):
        return tiles_all.at[dx * 2 + flip, i]

    def send_tiles(which):
        for n in which:
            for i, dx, sem in ((n, 1, 0), (blocks - 1 - n, NX - 1, 1)):
                remote(
                    tiles_ref.at[i], tile_slot(NX - dx, 0, i), t_send, t_recv.at[sem, i], (0, dx, 0)
                ).start()

    def share_tiles(dx, i):
        remote(
            tile_slot(dx, 0, i), tile_slot(dx, 1, i), t_send, t_sib.at[dx, i], (0, 0, 1)
        ).start()

    def pass_tiles(which):
        for n in which:
            for i, dx, sem in ((n, NX - 1, 0), (blocks - 1 - n, 1, 1)):
                land(tile_slot(dx, 0, i), t_recv.at[sem, i])
                if n < blocks // 2:
                    toward = 1 if sem == 0 else NX - 1
                    remote(
                        tile_slot(dx, 0, i), tile_slot(2, 0, i), t_send, t_far.at[i], (0, toward, 0)
                    ).start()
                share_tiles(dx, i)

    near = [(0, 0, 1)] + [p for p in row if p[1] != 0] + column
    metas[0, pl.ds(0, blocks), pl.ds(0, slots)] = cols_ref[...]
    metas[0, pl.ds(blocks, 1), pl.ds(0, chosen_ref.shape[1])] = chosen_ref[...]
    start_stage(0)
    for peer in near:
        dz, dx, f = peer
        if dz == 0:
            slot = ((NX - dx) % NX) * 2 + f
        else:
            slot = 2 * NX + (NZ - dz - 1) * 2 + f
        remote(metas.at[0], metas.at[slot], m_send, m_recv, peer).start()
    for i in range(blocks):
        remote(tiles_ref.at[i], tile_slot(0, 1, i), t_send, t_sib.at[0, i], (0, 0, 1)).start()
    send_tiles(range(blocks // 2))
    own_tiles = pltpu.make_async_copy(tiles_ref, tiles_all.at[0], t_own)
    own_tiles.start()
    for f in feats:
        f[2 * NZ * blocks] = jnp.zeros((size, wide), f.dtype)

    def copy_metas():
        land(metas.at[pl.ds(1, len(near))], m_recv)
        copy = pltpu.make_async_copy(metas, metas_smem, m_copy)
        copy.start()
        copy.wait()

    def build_table(readers):
        for reader in readers:
            dx, f = reader // 2, reader % 2
            reader_index = dom_index(my_z, lax.rem(my_x + dx, NX), other if f else core)

            def entry(n, carry):
                col = metas_smem[reader, n // slots, n % slots]
                owner = jnp.maximum(col - blocks, 0)
                valid = (col >= blocks) & ((owner // 2) % NX == my_x)
                dz = (owner // (2 * NX) - my_z + NZ) % NZ
                flip = (owner + core) % 2
                where = jnp.where(dz == 0, flip, 2 * NX + (dz - 1) * 2 + flip)
                block = metas_smem[where, blocks, reader_index]
                slot = (dz * 2 + flip) * blocks + block
                table[reader * blocks * slots + n] = jnp.where(valid, slot, 2 * NZ * blocks)
                return carry

            lax.fori_loop(0, blocks * slots, entry, 0)

    def build_local(i):
        sums = [jnp.zeros((size, size), f32) for _ in range(blocks)]
        for k in range(slots):
            tile = tiles_ref[i, k].astype(f32)
            for c in range(blocks):
                mask = jnp.where(metas_smem[0, i, k] == c, 1.0, 0.0).astype(f32)
                sums[c] += tile * mask
        for c in range(blocks):
            local_ref[pl.ds(i * size, size), pl.ds(c * size, size)] = sums[c].astype(bf16)

    def product(stage, reader, i):
        first = (reader * blocks + i) * slots
        left = jnp.concatenate([tiles_all[reader, i, k] for k in range(slots)], axis=1)
        right = jnp.concatenate([feats[stage][table[first + k]] for k in range(slots)], axis=0)
        return dot(left, right)

    def send_part(stage, reader, which=slice(None)):
        dx, f = reader // 2, reader % 2
        if dx == 2:
            toward = 1 if f == 0 else NX - 1
            remote(
                part_out.at[stage, reader, which], relay_in.at[stage, f, which],
                relay_send.at[stage], relay_recv.at[stage, f, 0 if which == slice(None) else which],
                (0, toward, 0),
            ).start()
        elif reader:
            source = {0: 0, 1: 2, NX - 1: 1}[dx]
            remote(
                part_out.at[stage, reader, which], part_in.at[stage, source * 2 + f, which],
                p_send.at[stage], p_recv.at[stage], (0, dx, f),
            ).start()

    def partial(stage, reader):
        dx, f = reader // 2, reader % 2
        relays = (dx, f) in ((1, 0), (NX - 1, 1))
        if relays:
            land(relay_in.at[stage, f], relay_recv.at[stage, f, 0])

        def one(i, carry):
            total = product(stage, reader, i)
            if relays:
                total += relay_in[stage, f, i].astype(f32)
            part_out[stage, reader, i] = total.astype(bf16)
            return carry

        lax.fori_loop(0, blocks, one, 0)
        send_part(stage, reader)

    def last_partials():
        stage = STAGES - 1
        for reader in (4, 5, 3, 6):
            totals = [product(stage, reader, i) for i in range(blocks)]
            for i in range(blocks):
                part_out[stage, reader, i] = totals[i].astype(bf16)
            if reader // 2 == 2:
                for i in range(blocks):
                    send_part(stage, reader, i)
            else:
                send_part(stage, reader)
        relayed = (2, 7)
        for reader in relayed:
            for i in range(blocks):
                relay_sum[reader % 2, i] = product(stage, reader, i)
        for i in range(blocks):
            for reader in relayed:
                f = reader % 2
                land(relay_in.at[stage, f, i], relay_recv.at[stage, f, i])
                total = relay_sum[f, i] + relay_in[stage, f, i].astype(f32)
                part_out[stage, reader, i] = total.astype(bf16)
                send_part(stage, reader, i)
        for reader in (1, 0):
            for i in range(blocks):
                part_out[stage, reader, i] = product(stage, reader, i).astype(bf16)
            send_part(stage, reader)

    def column_chunk(stage, flip):
        return (other if flip else core) * 2 + stage % 2

    def total_of(stage, flip):
        first = part_in[stage, 1] if flip else part_out[stage, 0]
        total = first.astype(f32)
        for source in (1, 2):
            total += part_in[stage, source * 2 + flip].astype(f32)
        return total.reshape(rows, wide)

    def received(stage):
        land(part_in.at[stage, pl.ds(1, 5)], p_recv.at[stage])

    def finish_one(stage):
        received(stage)
        for flip in range(2):
            received_ref[column_chunk(stage, flip)] = total_of(stage, flip)

    def layer_one(i):
        here = pl.ds(i * size, size)
        local = local_ref[here, :]
        own = initial_ref[...].reshape(rows, width)
        got = jnp.concatenate([received_ref[q, here, :] for q in range(4)], axis=1)
        mixed = (
            (1.0 - RESTART) * (dot(local, own) + got) + RESTART * initial_ref[i].astype(f32)
        ).astype(bf16)
        pre = (1.0 - BETA_ONE) * mixed.astype(f32) + BETA_ONE * dot(mixed, one_ref[...])
        sig = sigmoid(pre)
        mixed_one_ref[here, :] = mixed
        hidden_ref[here, :] = (pre * sig).astype(bf16)
        slope_ref[here, :] = sig * (1.0 + pre * (1.0 - sig))

    def start_two():
        total = (1.0 - RESTART) * dot(local_ref[...], hidden_ref[...]) + RESTART * initial_ref[
            ...
        ].reshape(rows, width).astype(f32)
        for q in range(4):
            base_ref[q] = total[:, q * wide : (q + 1) * wide]

    def finish_two(stage):
        received(stage)
        for flip in range(2):
            chunk = column_chunk(stage, flip)
            mixed = base_ref[chunk] + (1.0 - RESTART) * total_of(stage, flip)
            mixed_two_ref[:, pl.ds(pl.multiple_of(chunk * wide, wide), wide)] = mixed.astype(bf16)

    def store_grad(g, grad):
        grad_ref[g] = grad
        send_ref[g] = grad.astype(bf16)

    def layer_two():
        mixed_two = mixed_two_ref[...]
        pre_two = (1.0 - BETA_TWO) * mixed_two.astype(f32) + BETA_TWO * dot(mixed_two, two_ref[...])
        sig = sigmoid(pre_two)
        out_ref[...] = (pre_two * sig).astype(bf16)
        slope_two = sig * (1.0 + pre_two * (1.0 - sig))
        back_two = (cot_ref[...].astype(f32) * slope_two).astype(bf16)
        back_mixed = (
            (1.0 - BETA_TWO) * back_two.astype(f32)
            + BETA_TWO * dot(back_two, two_ref[...], ((1,), (1,)))
        ).astype(bf16)
        back_hidden = (1.0 - RESTART) * dot(local_ref[...], back_mixed, ((0,), (0,)))
        back_one = (back_hidden * slope_ref[...]).astype(bf16)
        store_grad(1, dot(mixed_two, back_two, ((0,), (0,))))
        store_grad(0, dot(mixed_one_ref[...], back_one, ((0,), (0,))))

    turns = {(stage, m): [] for stage in range(STAGES) for m in range(NZ - 1)}
    for m, dx, f in ((0, 0, 1), (1, 0, 0), (2, 1, 1), (3, 3, 0), (5, 2, 0), (6, 2, 1)):
        turns[1, m].append((0, dx, f))
    turns[2, 2].append((0, 1, 0))
    turns[2, 3].append((0, 3, 1))
    order = [(2, 0), (2, 1), (1, 1), (3, 0), (1, 0), (3, 1), (0, 1), (0, 0)]
    for stage in range(2, STAGES):
        for turn, (dx, f) in enumerate(order):
            turns[stage, min(turn, NZ - 2)].append((stage - 1, dx, f))

    for stage in range(STAGES):
        for m in range(NZ - 1):
            ring_tick(stage, m)
            if m == 4 and stage + 1 < STAGES:
                start_stage(stage + 1)
            if stage == 0:
                if m == 1:
                    send_tiles(range(blocks // 2, blocks))
                    copy_metas()
                if m >= 2 and m < 6:
                    build_table((2 * (m - 2), 2 * (m - 2) + 1))
                    build_local(m - 2)
                if m == 5:
                    pass_tiles(range(blocks // 2))
                continue
            if stage == 1:
                if m == 0:
                    own_tiles.wait()
                    for i in range(blocks):
                        land(tile_slot(0, 1, i), t_sib.at[0, i])
                if m == 1:
                    pass_tiles(range(blocks // 2, blocks))
                if m == 2:
                    for i in range(blocks):
                        land(tile_slot(1, 1, i), t_sib.at[1, i])
                        land(tile_slot(NX - 1, 1, i), t_sib.at[NX - 1, i])
                if m == 5:
                    for i in range(blocks):
                        land(tile_slot(2, 0, i), t_far.at[i])
                        share_tiles(2, i)
                if m == 6:
                    for i in range(blocks):
                        land(tile_slot(2, 1, i), t_sib.at[2, i])
            for of, dx, f in turns[stage, m]:
                partial(of, dx * 2 + f)
        land(feat_slot(stage, 0, 1), sib_recv.at[stage])
        land(feat_slot(stage, 0, 0), own_sem.at[stage])
    last_partials()
    for stage in range(2):
        finish_one(stage)
    for i in range(blocks):
        layer_one(i)
    start_two()
    finish_two(2)
    finish_two(3)
    layer_two()

    remote(send_ref.at[other], pair_in, pair_sems.at[0], pair_sems.at[1], (0, 0, 1)).start()
    land(pair_in, pair_sems.at[1])
    pair_sum[...] = (grad_ref[core] + pair_in[...].astype(f32)).astype(bf16)

    half = width // 2
    quarter = half // NX
    part = quarter // NX
    place = ((my_x, my_y), (my_y, my_x))

    def rows_at(start, count):
        return pl.ds(pl.multiple_of(start, part), count)

    def along(h, turn, d):
        return (0, d, 0) if h == turn else (0, 0, 0, d)

    for d in (2, 1, 3):
        for h in range(2):
            theirs = rows_at(h * half + lax.rem(place[h][0] + d, NX) * quarter, quarter)
            remote(
                pair_sum.at[theirs], first_in.at[h, NX - d - 1],
                first_send, first_recv.at[h], along(h, 0, d),
            ).start()
    for h in range(2):
        mine = rows_at(h * half + place[h][0] * quarter, quarter)
        value = grad_ref[core, mine, :] + pair_in[mine, :].astype(f32)
        land(first_in.at[h], first_recv.at[h])
        for n in range(NX - 1):
            value += first_in[h, n].astype(f32)
        first_sum[h] = value
        first_out[h] = value.astype(bf16)
        for d in (2, 1, 3):
            theirs = rows_at(lax.rem(place[h][1] + d, NX) * part, part)
            remote(
                first_out.at[h, theirs], second_in.at[h, NX - d - 1],
                second_send, second_recv.at[h], along(h, 1, d),
            ).start()
    tiles_of = [(r, q) for r in range(part // 8) for q in range(4)]
    for h in range(2):
        value = first_sum[h, rows_at(place[h][1] * part, part), :]
        land(second_in.at[h], second_recv.at[h])
        for n in range(NX - 1):
            value += second_in[h, n].astype(f32)
        for n, (r, q) in enumerate(tiles_of):
            third[n, h] = value[r * 8 : (r + 1) * 8, q * wide : (q + 1) * wide]
    for dz in (4, 3, 5, 2, 6, 1, 7):
        remote(
            third.at[lax.rem(my_z + dz, NZ)], third_in.at[NZ - dz - 1],
            third_send, third_recv, (dz, 0, 0),
        ).start()
    value = third[my_z]
    land(third_in, third_recv)
    for n in range(NZ - 1):
        value += third_in[n]
    third_done[my_z] = value
    for dz in (4, 3, 5, 2, 6, 1, 7):
        remote(
            third_done.at[my_z], third_done.at[my_z], done_send, done_recv, (dz, 0, 0)
        ).start()
    land(third_done.at[pl.ds(0, NZ - 1)], done_recv)

    for h in range(2):
        value = jnp.concatenate(
            [
                jnp.concatenate([third_done[r * 4 + q, h] for q in range(4)], axis=1)
                for r in range(part // 8)
            ],
            axis=0,
        )
        mine = rows_at(h * half + place[h][0] * quarter + place[h][1] * part, part)
        sum_ref[core, mine, :] = value.astype(bf16)
        for d in (2, 1, 3):
            remote(
                sum_ref.at[core, mine], sum_ref.at[core, mine],
                gather_send, gather_recv.at[h], along(h, 1, d),
            ).start()
    for h in range(2):
        land(second_in.at[h], gather_recv.at[h])
        mine = rows_at(h * half + place[h][0] * quarter, quarter)
        for d in (2, 1, 3):
            remote(
                sum_ref.at[core, mine], sum_ref.at[core, mine],
                share_send, share_recv.at[h, NX - d - 1], along(h, 0, d),
            ).start()
        remote(
            sum_ref.at[core, mine], sum_ref.at[core, mine],
            back_send, back_recv.at[h, 0], (0, 0, 1),
        ).start()

    def share_at(h, d):
        return rows_at(h * half + lax.rem(place[h][0] + d, NX) * quarter, quarter)

    for d in (1, 3, 2):
        for h in range(2):
            got = share_at(h, d)
            land(sum_ref.at[core, got], share_recv.at[h, d - 1])
            remote(
                sum_ref.at[core, got], sum_ref.at[core, got],
                back_send, back_recv.at[h, d], (0, 0, 1),
            ).start()
    for d in range(NX):
        for h in range(2):
            land(sum_ref.at[other, share_at(h, d)], back_recv.at[h, d])

    for stage in range(STAGES):
        land(feats[stage].at[pl.ds(0, 15 * blocks)], z_send.at[stage])
        land(part_in.at[stage, pl.ds(1, 5)], p_send.at[stage])
        land(relay_in.at[stage], relay_send.at[stage])
    land(metas.at[pl.ds(1, len(near))], m_send)
    land(tiles_all.at[pl.ds(1, 2 * NX - 1)], t_send)
    land(pair_in, pair_sems.at[0])
    land(first_in, first_send)
    land(second_in, second_send)
    land(third_in, third_send)
    land(third_in, done_send)
    land(second_in, gather_send)
    land(first_in, share_send)
    land(pair_in, back_send)


def layers(initial, history, tiles, cols, chosen, weight_one, weight_two, cotangent):
    blocks, size, width = initial.shape
    slots = tiles.shape[1]
    wide = width // 4
    rows = blocks * size
    quarter = width // 2 // NX
    part = quarter // NX
    vmem = pl.BlockSpec(memory_space=pltpu.VMEM)
    dma = pltpu.SemaphoreType.DMA
    bf16 = jnp.bfloat16
    f32 = jnp.float32
    metas = 2 * NX + 2 * (NZ - 1)
    return pl.pallas_call(
        layers_kernel,
        out_shape=(
            jax.ShapeDtypeStruct((rows, width), bf16),
            jax.ShapeDtypeStruct((2, width, width), bf16),
        ),
        in_specs=[vmem] * 8,
        out_specs=(vmem, vmem),
        scratch_shapes=[pltpu.VMEM((2 * NZ * blocks + 1, size, wide), bf16)] * STAGES
        + [
            pltpu.VMEM((2 * NX, blocks, slots, size, size), bf16),
            pltpu.VMEM((STAGES, 2 * NX, blocks, size, wide), bf16),
            pltpu.VMEM((STAGES, 6, blocks, size, wide), bf16),
            pltpu.VMEM((STAGES, 2, blocks, size, wide), bf16),
            pltpu.VMEM((2, blocks, size, wide), f32),
            pltpu.VMEM((metas, 8, 128), jnp.int32),
            pltpu.SMEM((metas, 8, 128), jnp.int32),
            pltpu.SMEM((2 * NX * blocks * slots,), jnp.int32),
            pltpu.VMEM((rows, rows), bf16),
            pltpu.VMEM((4, rows, wide), f32),
            pltpu.VMEM((4, rows, wide), f32),
            pltpu.VMEM((rows, width), bf16),
            pltpu.VMEM((rows, width), bf16),
            pltpu.VMEM((rows, width), bf16),
            pltpu.VMEM((rows, width), f32),
            pltpu.VMEM((2, width, width), f32),
            pltpu.VMEM((2, width, width), bf16),
            pltpu.VMEM((width, width), bf16),
            pltpu.VMEM((width, width), bf16),
            pltpu.VMEM((2, NX - 1, quarter, width), bf16),
            pltpu.VMEM((2, quarter, width), f32),
            pltpu.VMEM((2, quarter, width), bf16),
            pltpu.VMEM((2, NX - 1, part, width), bf16),
            pltpu.VMEM((NZ, 2, 8, wide), f32),
            pltpu.VMEM((NZ - 1, 2, 8, wide), f32),
            pltpu.VMEM((NZ, 2, 8, wide), f32),
            dma((STAGES, 2, NZ - 1)),
            dma((STAGES,)),
            dma((STAGES,)),
            dma((STAGES,)),
            dma((2, blocks)),
            dma((blocks,)),
            dma((NX, blocks)),
            dma,
            dma,
            dma((STAGES,)),
            dma((STAGES,)),
            dma((STAGES, 2, blocks)),
            dma((STAGES,)),
            dma,
            dma,
            dma,
            dma((2,)),
            dma,
            dma((2,)),
            dma,
            dma((2,)),
            dma,
            dma,
            dma,
            dma,
            dma,
            dma((2,)),
            dma,
            dma((2, NX - 1)),
            dma,
            dma((2, NX)),
        ],
        compiler_params=pltpu.CompilerParams(
            collective_id=0, has_side_effects=True, vmem_limit_bytes=56 * 2**20
        ),
        cost_estimate=pl.CostEstimate(
            flops=7 * 10**9, bytes_accessed=8 * 2**20, transcendentals=2**19
        ),
        name="layers",
    )(initial, history, tiles, cols, chosen, weight_one, weight_two, cotangent)


def local(initial, history, tile_values, tile_cols, send_blocks, weight_one, weight_two, cotangent):
    tiles = tile_values[0]
    blocks, slots, size, _ = tiles.shape
    width = initial.shape[2]
    output, summed = layers(
        initial[0].reshape(blocks, size, width), history[0].reshape(blocks, size, width),
        tiles, tile_cols[0], send_blocks[0], weight_one, weight_two, cotangent[0],
    )
    grad_one = BETA_ONE * summed[0].astype(jnp.float32)
    grad_two = BETA_TWO * summed[1].astype(jnp.float32)
    return (output[None], grad_one, grad_two)


def solution(mesh):
    return jax.shard_map(
        local,
        mesh=mesh,
        in_specs=(
            P("grp", "dom", None),
            P("grp", "dom", None),
            P("grp", "dom", None, None, None),
            P("grp", "dom", None),
            P("grp", "dom", None),
            P(),
            P(),
            P("grp", "dom", None),
        ),
        out_specs=(P("grp", "dom", None), P(), P()),
        check_vma=False,
    )
```

```python
import functools

import jax
import jax.numpy as jnp
from jax import lax
from jax.experimental import pallas as pl
from jax.experimental.pallas import tpu as pltpu
from jax.sharding import PartitionSpec as P

RESTART = 0.1
BETA_ONE = 0.405465
BETA_TWO = 0.223144

NZ = 8
NX = 4
NY = 4
STAGES = 4
MESH = pl.DeviceIdType.MESH


def dom_index(z, x, core):
    return (z * NX + x) * 2 + core


def sigmoid(value):
    return 1.0 / (1.0 + jnp.exp(-value))


def dot(a, b, dims=((1,), (0,))):
    return lax.dot_general(a, b, (dims, ((), ())), preferred_element_type=jnp.float32)


def layers_kernel(
    initial_ref, history_ref, tiles_ref, cols_ref, chosen_ref, one_ref, two_ref, cot_ref,
    out_ref, sum_ref,
    feat0, feat1, feat2, feat3, tiles_all, part_out, part_in, relay_in, relay_sum, metas, metas_smem, table,
    local_ref, base_ref, received_ref, mixed_one_ref, mixed_two_ref, hidden_ref, slope_ref,
    grad_ref, send_ref, pair_in, pair_sum, first_in, first_sum, first_out, second_in,
    third, third_in, third_done,
    z_recv, sib_recv, z_send, own_sem, t_recv, t_far, t_sib, t_send, t_own, p_recv, p_send,
    relay_recv, relay_send, m_recv, m_send, m_copy, pair_sems, first_send, first_recv,
    second_send, second_recv, third_send, third_recv, done_send, done_recv,
    gather_send, gather_recv, share_send, share_recv, back_send, back_recv,
):
    f32 = jnp.float32
    bf16 = jnp.bfloat16
    feats = (feat0, feat1, feat2, feat3)
    blocks, size, width = initial_ref.shape
    slots = tiles_ref.shape[1]
    wide = feat0.shape[2]
    rows = blocks * size
    dom = lax.axis_index("dom")
    my_y = lax.axis_index("grp")
    core = lax.rem(dom, 2)
    my_x = lax.rem(dom // 2, NX)
    my_z = dom // (2 * NX)
    other = 1 - core

    def at(dz, dx, flip, dy=0):
        z = lax.rem(my_z + dz, NZ)
        x = lax.rem(my_x + dx, NX)
        y = lax.rem(my_y + dy, NY)
        return (dom_index(z, x, other if flip else core), y)

    row = [(0, dx, f) for dx in range(NX) for f in range(2) if (dx, f) != (0, 0)]
    column = [(dz, 0, f) for dz in range(1, NZ) for f in range(2)]
    stack = [(0, 0, 0, dy) for dy in range(1, NY)]
    barrier = pltpu.get_barrier_semaphore()
    for peer in row + column + stack:
        pl.semaphore_signal(barrier, inc=1, device_id=at(*peer), device_id_type=MESH)
    pl.semaphore_wait(barrier, len(row) + len(column) + len(stack))

    def remote(src, dst, send_sem, recv_sem, peer):
        return pltpu.make_async_remote_copy(
            src_ref=src, dst_ref=dst, send_sem=send_sem, recv_sem=recv_sem,
            device_id=at(*peer), device_id_type=MESH,
        )

    def land(ref, sem):
        pltpu.make_async_copy(ref, ref, sem).wait()

    def feat_slot(stage, dz, flip):
        return feats[stage].at[pl.ds((dz * 2 + flip) * blocks, blocks)]

    def own_columns(stage, flip):
        ref = (initial_ref, history_ref)[stage // 2]
        half = other if flip else core
        start = pl.multiple_of((half * 2 + stage % 2) * wide, wide)
        return ref.at[:, :, pl.ds(start, wide)]

    def start_stage(stage):
        for flip in range(2):
            for direction, dz in ((0, 1), (1, NZ - 1)):
                remote(
                    own_columns(stage, flip), feat_slot(stage, NZ - dz, flip),
                    z_send.at[stage], z_recv.at[stage, direction, flip], (dz, 0, flip),
                ).start()
        remote(
            own_columns(stage, 1), feat_slot(stage, 0, 1),
            z_send.at[stage], sib_recv.at[stage], (0, 0, 1),
        ).start()
        pltpu.make_async_copy(own_columns(stage, 0), feat_slot(stage, 0, 0), own_sem.at[stage]).start()

    def ring_tick(stage, m):
        for direction, dz in ((0, 1), (1, NZ - 1)):
            hop = m // 2 + 1
            flip = m % 2 if hop < NZ // 2 else direction
            origin = (NZ - hop if direction == 0 else hop) % NZ
            slot = feat_slot(stage, origin, flip)
            land(slot, z_recv.at[stage, direction, m])
            if hop < NZ // 2 - 1 or (hop == NZ // 2 - 1 and flip == direction):
                later = m + 2 if hop < NZ // 2 - 1 else NZ - 2
                next_origin = (NZ - hop - 1 if direction == 0 else hop + 1) % NZ
                remote(
                    slot, feat_slot(stage, next_origin, flip),
                    z_send.at[stage], z_recv.at[stage, direction, later], (dz, 0, 0),
                ).start()

    def tile_slot(dx, flip, i):
        return tiles_all.at[dx * 2 + flip, i]

    def send_tiles(which):
        for n in which:
            for i, dx, sem in ((n, 1, 0), (blocks - 1 - n, NX - 1, 1)):
                remote(
                    tiles_ref.at[i], tile_slot(NX - dx, 0, i), t_send, t_recv.at[sem, i], (0, dx, 0)
                ).start()

    def share_tiles(dx, i):
        remote(
            tile_slot(dx, 0, i), tile_slot(dx, 1, i), t_send, t_sib.at[dx, i], (0, 0, 1)
        ).start()

    def pass_tiles(which):
        for n in which:
            for i, dx, sem in ((n, NX - 1, 0), (blocks - 1 - n, 1, 1)):
                land(tile_slot(dx, 0, i), t_recv.at[sem, i])
                if n < blocks // 2:
                    toward = 1 if sem == 0 else NX - 1
                    remote(
                        tile_slot(dx, 0, i), tile_slot(2, 0, i), t_send, t_far.at[i], (0, toward, 0)
                    ).start()
                share_tiles(dx, i)

    near = [(0, 0, 1)] + [p for p in row if p[1] != 0] + column
    metas[0, pl.ds(0, blocks), pl.ds(0, slots)] = cols_ref[...]
    metas[0, pl.ds(blocks, 1), pl.ds(0, chosen_ref.shape[1])] = chosen_ref[...]
    start_stage(0)
    for peer in near:
        dz, dx, f = peer
        if dz == 0:
            slot = ((NX - dx) % NX) * 2 + f
        else:
            slot = 2 * NX + (NZ - dz - 1) * 2 + f
        remote(metas.at[0], metas.at[slot], m_send, m_recv, peer).start()
    for i in range(blocks):
        remote(tiles_ref.at[i], tile_slot(0, 1, i), t_send, t_sib.at[0, i], (0, 0, 1)).start()
    send_tiles(range(blocks // 2))
    own_tiles = pltpu.make_async_copy(tiles_ref, tiles_all.at[0], t_own)
    own_tiles.start()
    for f in feats:
        f[2 * NZ * blocks] = jnp.zeros((size, wide), f.dtype)

    def copy_metas():
        land(metas.at[pl.ds(1, len(near))], m_recv)
        copy = pltpu.make_async_copy(metas, metas_smem, m_copy)
        copy.start()
        copy.wait()

    def build_table(readers):
        for reader in readers:
            dx, f = reader // 2, reader % 2
            reader_index = dom_index(my_z, lax.rem(my_x + dx, NX), other if f else core)

            def entry(n, carry):
                col = metas_smem[reader, lax.div(n, slots), lax.rem(n, slots)]
                owner = jnp.maximum(col - blocks, 0)
                chip = lax.div(owner, 2)
                valid = (col >= blocks) & (lax.rem(chip, NX) == my_x)
                dz = lax.rem(lax.div(chip, NX) + (NZ - my_z), NZ)
                flip = lax.rem(owner + core, 2)
                place = dz * 2 + flip
                where = jnp.where(dz == 0, flip, place + (2 * NX - 2))
                block = metas_smem[where, blocks, reader_index]
                slot = place * blocks + block
                table[reader * blocks * slots + n] = jnp.where(valid, slot, 2 * NZ * blocks)
                return carry

            lax.fori_loop(0, blocks * slots, entry, 0, unroll=slots)

    def build_local(i):
        sums = [jnp.zeros((size, size), f32) for _ in range(blocks)]
        for k in range(slots):
            tile = tiles_ref[i, k].astype(f32)
            for c in range(blocks):
                mask = jnp.where(metas_smem[0, i, k] == c, 1.0, 0.0).astype(f32)
                sums[c] += tile * mask
        for c in range(blocks):
            local_ref[pl.ds(i * size, size), pl.ds(c * size, size)] = sums[c].astype(bf16)

    def product(stage, reader, i):
        first = (reader * blocks + i) * slots
        left = jnp.concatenate([tiles_all[reader, i, k] for k in range(slots)], axis=1)
        right = jnp.concatenate([feats[stage][table[first + k]] for k in range(slots)], axis=0)
        return dot(left, right)

    def send_part(stage, reader, which=slice(None)):
        dx, f = reader // 2, reader % 2
        if dx == 2:
            toward = 1 if f == 0 else NX - 1
            remote(
                part_out.at[stage, reader, which], relay_in.at[stage, f, which],
                relay_send.at[stage], relay_recv.at[stage, f, 0 if which == slice(None) else which],
                (0, toward, 0),
            ).start()
        elif reader:
            source = {0: 0, 1: 2, NX - 1: 1}[dx]
            remote(
                part_out.at[stage, reader, which], part_in.at[stage, source * 2 + f, which],
                p_send.at[stage], p_recv.at[stage], (0, dx, f),
            ).start()

    def partial(stage, reader):
        dx, f = reader // 2, reader % 2
        relays = (dx, f) in ((1, 0), (NX - 1, 1))
        if relays:
            land(relay_in.at[stage, f], relay_recv.at[stage, f, 0])

        def one(i, carry):
            total = product(stage, reader, i)
            if relays:
                total += relay_in[stage, f, i].astype(f32)
            part_out[stage, reader, i] = total.astype(bf16)
            return carry

        lax.fori_loop(0, blocks, one, 0)
        send_part(stage, reader)

    def last_partials():
        stage = STAGES - 1
        for reader in (4, 5, 3, 6):
            totals = [product(stage, reader, i) for i in range(blocks)]
            for i in range(blocks):
                part_out[stage, reader, i] = totals[i].astype(bf16)
            if reader // 2 == 2:
                for i in range(blocks):
                    send_part(stage, reader, i)
            else:
                send_part(stage, reader)
        relayed = (2, 7)
        for reader in relayed:
            for i in range(blocks):
                relay_sum[reader % 2, i] = product(stage, reader, i)
        for i in range(blocks):
            for reader in relayed:
                f = reader % 2
                land(relay_in.at[stage, f, i], relay_recv.at[stage, f, i])
                total = relay_sum[f, i] + relay_in[stage, f, i].astype(f32)
                part_out[stage, reader, i] = total.astype(bf16)
                send_part(stage, reader, i)
        for reader in (1, 0):
            for i in range(blocks):
                part_out[stage, reader, i] = product(stage, reader, i).astype(bf16)
            send_part(stage, reader)

    def column_chunk(stage, flip):
        return (other if flip else core) * 2 + stage % 2

    def total_of(stage, flip):
        first = part_in[stage, 1] if flip else part_out[stage, 0]
        total = first.astype(f32)
        for source in (1, 2):
            total += part_in[stage, source * 2 + flip].astype(f32)
        return total.reshape(rows, wide)

    def received(stage):
        land(part_in.at[stage, pl.ds(1, 5)], p_recv.at[stage])

    def finish_one(stage):
        received(stage)
        for flip in range(2):
            received_ref[column_chunk(stage, flip)] = total_of(stage, flip)

    def layer_one(i):
        here = pl.ds(i * size, size)
        local = local_ref[here, :]
        own = initial_ref[...].reshape(rows, width)
        got = jnp.concatenate([received_ref[q, here, :] for q in range(4)], axis=1)
        mixed = (
            (1.0 - RESTART) * (dot(local, own) + got) + RESTART * initial_ref[i].astype(f32)
        ).astype(bf16)
        pre = (1.0 - BETA_ONE) * mixed.astype(f32) + BETA_ONE * dot(mixed, one_ref[...])
        sig = sigmoid(pre)
        mixed_one_ref[here, :] = mixed
        hidden_ref[here, :] = (pre * sig).astype(bf16)
        slope_ref[here, :] = sig * (1.0 + pre * (1.0 - sig))

    def start_two():
        total = (1.0 - RESTART) * dot(local_ref[...], hidden_ref[...]) + RESTART * initial_ref[
            ...
        ].reshape(rows, width).astype(f32)
        for q in range(4):
            base_ref[q] = total[:, q * wide : (q + 1) * wide]

    def finish_two(stage):
        received(stage)
        for flip in range(2):
            chunk = column_chunk(stage, flip)
            mixed = base_ref[chunk] + (1.0 - RESTART) * total_of(stage, flip)
            mixed_two_ref[:, pl.ds(pl.multiple_of(chunk * wide, wide), wide)] = mixed.astype(bf16)

    def store_grad(g, grad):
        grad_ref[g] = grad
        send_ref[g] = grad.astype(bf16)

    def layer_two():
        mixed_two = mixed_two_ref[...]
        pre_two = (1.0 - BETA_TWO) * mixed_two.astype(f32) + BETA_TWO * dot(mixed_two, two_ref[...])
        sig = sigmoid(pre_two)
        out_ref[...] = (pre_two * sig).astype(bf16)
        slope_two = sig * (1.0 + pre_two * (1.0 - sig))
        back_two = (cot_ref[...].astype(f32) * slope_two).astype(bf16)
        back_mixed = (
            (1.0 - BETA_TWO) * back_two.astype(f32)
            + BETA_TWO * dot(back_two, two_ref[...], ((1,), (1,)))
        ).astype(bf16)
        back_hidden = (1.0 - RESTART) * dot(local_ref[...], back_mixed, ((0,), (0,)))
        back_one = (back_hidden * slope_ref[...]).astype(bf16)
        store_grad(1, dot(mixed_two, back_two, ((0,), (0,))))
        store_grad(0, dot(mixed_one_ref[...], back_one, ((0,), (0,))))

    turns = {(stage, m): [] for stage in range(STAGES) for m in range(NZ - 1)}
    for m, dx, f in ((0, 0, 1), (1, 0, 0), (2, 1, 1), (3, 3, 0), (5, 2, 0), (6, 2, 1)):
        turns[1, m].append((0, dx, f))
    turns[2, 2].append((0, 1, 0))
    turns[2, 3].append((0, 3, 1))
    order = [(2, 0), (2, 1), (1, 1), (3, 0), (1, 0), (3, 1), (0, 1), (0, 0)]
    for stage in range(2, STAGES):
        for turn, (dx, f) in enumerate(order):
            turns[stage, min(turn, NZ - 2)].append((stage - 1, dx, f))

    for stage in range(STAGES):
        for m in range(NZ - 1):
            ring_tick(stage, m)
            if m == 5 and stage + 1 < STAGES:
                start_stage(stage + 1)
            if stage == 0:
                if m == 1:
                    send_tiles(range(blocks // 2, blocks))
                    copy_metas()
                if m in (2, 3, 4, 6):
                    build_table({2: (1, 0), 3: (3, 6), 4: (4, 5), 6: (2, 7)}[m])
                if m == 5:
                    pass_tiles(range(blocks // 2))
                continue
            if stage == 1:
                if m == 0:
                    own_tiles.wait()
                    for i in range(blocks):
                        land(tile_slot(0, 1, i), t_sib.at[0, i])
                if m == 1:
                    pass_tiles(range(blocks // 2, blocks))
                if m == 2:
                    for i in range(blocks):
                        land(tile_slot(1, 1, i), t_sib.at[1, i])
                        land(tile_slot(NX - 1, 1, i), t_sib.at[NX - 1, i])
                if m == 5:
                    for i in range(blocks):
                        land(tile_slot(2, 0, i), t_far.at[i])
                        share_tiles(2, i)
                if m == 6:
                    for i in range(blocks):
                        land(tile_slot(2, 1, i), t_sib.at[2, i])
            for of, dx, f in turns[stage, m]:
                partial(of, dx * 2 + f)
        land(feat_slot(stage, 0, 1), sib_recv.at[stage])
        land(feat_slot(stage, 0, 0), own_sem.at[stage])
    last_partials()
    for stage in range(2):
        finish_one(stage)
    for i in range(blocks):
        build_local(i)
        layer_one(i)
    start_two()
    finish_two(2)
    finish_two(3)
    layer_two()

    remote(send_ref.at[other], pair_in, pair_sems.at[0], pair_sems.at[1], (0, 0, 1)).start()
    land(pair_in, pair_sems.at[1])
    pair_sum[...] = (grad_ref[core] + pair_in[...].astype(f32)).astype(bf16)

    half = width // 2
    quarter = half // NX
    part = quarter // NX
    place = ((my_x, my_y), (my_y, my_x))

    def rows_at(start, count):
        return pl.ds(pl.multiple_of(start, part), count)

    def along(h, turn, d):
        return (0, d, 0) if h == turn else (0, 0, 0, d)

    for d in (2, 1, 3):
        for h in range(2):
            theirs = rows_at(h * half + lax.rem(place[h][0] + d, NX) * quarter, quarter)
            remote(
                pair_sum.at[theirs], first_in.at[h, NX - d - 1],
                first_send, first_recv.at[h], along(h, 0, d),
            ).start()
    for h in range(2):
        mine = rows_at(h * half + place[h][0] * quarter, quarter)
        value = grad_ref[core, mine, :] + pair_in[mine, :].astype(f32)
        land(first_in.at[h], first_recv.at[h])
        for n in range(NX - 1):
            value += first_in[h, n].astype(f32)
        first_sum[h] = value
        first_out[h] = value.astype(bf16)
        for d in (2, 1, 3):
            theirs = rows_at(lax.rem(place[h][1] + d, NX) * part, part)
            remote(
                first_out.at[h, theirs], second_in.at[h, NX - d - 1],
                second_send, second_recv.at[h], along(h, 1, d),
            ).start()
    tiles_of = [(r, q) for r in range(part // 8) for q in range(4)]
    for h in range(2):
        value = first_sum[h, rows_at(place[h][1] * part, part), :]
        land(second_in.at[h], second_recv.at[h])
        for n in range(NX - 1):
            value += second_in[h, n].astype(f32)
        for n, (r, q) in enumerate(tiles_of):
            third[n, h] = value[r * 8 : (r + 1) * 8, q * wide : (q + 1) * wide]
    for dz in (4, 3, 5, 2, 6, 1, 7):
        remote(
            third.at[lax.rem(my_z + dz, NZ)], third_in.at[NZ - dz - 1],
            third_send, third_recv, (dz, 0, 0),
        ).start()
    value = third[my_z]
    land(third_in, third_recv)
    for n in range(NZ - 1):
        value += third_in[n]
    third_done[my_z] = value
    for dz in (4, 3, 5, 2, 6, 1, 7):
        remote(
            third_done.at[my_z], third_done.at[my_z], done_send, done_recv, (dz, 0, 0)
        ).start()
    land(third_done.at[pl.ds(0, NZ - 1)], done_recv)

    for h in range(2):
        value = jnp.concatenate(
            [
                jnp.concatenate([third_done[r * 4 + q, h] for q in range(4)], axis=1)
                for r in range(part // 8)
            ],
            axis=0,
        )
        mine = rows_at(h * half + place[h][0] * quarter + place[h][1] * part, part)
        sum_ref[core, mine, :] = value.astype(bf16)
        for d in (2, 1, 3):
            remote(
                sum_ref.at[core, mine], sum_ref.at[core, mine],
                gather_send, gather_recv.at[h], along(h, 1, d),
            ).start()
    for h in range(2):
        land(second_in.at[h], gather_recv.at[h])
        mine = rows_at(h * half + place[h][0] * quarter, quarter)
        for d in (2, 1, 3):
            remote(
                sum_ref.at[core, mine], sum_ref.at[core, mine],
                share_send, share_recv.at[h, NX - d - 1], along(h, 0, d),
            ).start()
        remote(
            sum_ref.at[core, mine], sum_ref.at[core, mine],
            back_send, back_recv.at[h, 0], (0, 0, 1),
        ).start()

    def share_at(h, d):
        return rows_at(h * half + lax.rem(place[h][0] + d, NX) * quarter, quarter)

    for d in (1, 3, 2):
        for h in range(2):
            got = share_at(h, d)
            land(sum_ref.at[core, got], share_recv.at[h, d - 1])
            remote(
                sum_ref.at[core, got], sum_ref.at[core, got],
                back_send, back_recv.at[h, d], (0, 0, 1),
            ).start()
    for d in range(NX):
        for h in range(2):
            land(sum_ref.at[other, share_at(h, d)], back_recv.at[h, d])

    for stage in range(STAGES):
        land(feats[stage].at[pl.ds(0, 15 * blocks)], z_send.at[stage])
        land(part_in.at[stage, pl.ds(1, 5)], p_send.at[stage])
        land(relay_in.at[stage], relay_send.at[stage])
    land(metas.at[pl.ds(1, len(near))], m_send)
    land(tiles_all.at[pl.ds(1, 2 * NX - 1)], t_send)
    land(pair_in, pair_sems.at[0])
    land(first_in, first_send)
    land(second_in, second_send)
    land(third_in, third_send)
    land(third_in, done_send)
    land(second_in, gather_send)
    land(first_in, share_send)
    land(pair_in, back_send)


def layers(initial, history, tiles, cols, chosen, weight_one, weight_two, cotangent):
    blocks, size, width = initial.shape
    slots = tiles.shape[1]
    wide = width // 4
    rows = blocks * size
    quarter = width // 2 // NX
    part = quarter // NX
    vmem = pl.BlockSpec(memory_space=pltpu.VMEM)
    dma = pltpu.SemaphoreType.DMA
    bf16 = jnp.bfloat16
    f32 = jnp.float32
    metas = 2 * NX + 2 * (NZ - 1)
    return pl.pallas_call(
        layers_kernel,
        out_shape=(
            jax.ShapeDtypeStruct((rows, width), bf16),
            jax.ShapeDtypeStruct((2, width, width), bf16),
        ),
        in_specs=[vmem] * 8,
        out_specs=(vmem, vmem),
        scratch_shapes=[pltpu.VMEM((2 * NZ * blocks + 1, size, wide), bf16)] * STAGES
        + [
            pltpu.VMEM((2 * NX, blocks, slots, size, size), bf16),
            pltpu.VMEM((STAGES, 2 * NX, blocks, size, wide), bf16),
            pltpu.VMEM((STAGES, 6, blocks, size, wide), bf16),
            pltpu.VMEM((STAGES, 2, blocks, size, wide), bf16),
            pltpu.VMEM((2, blocks, size, wide), f32),
            pltpu.VMEM((metas, 8, 128), jnp.int32),
            pltpu.SMEM((metas, 8, 128), jnp.int32),
            pltpu.SMEM((2 * NX * blocks * slots,), jnp.int32),
            pltpu.VMEM((rows, rows), bf16),
            pltpu.VMEM((4, rows, wide), f32),
            pltpu.VMEM((4, rows, wide), f32),
            pltpu.VMEM((rows, width), bf16),
            pltpu.VMEM((rows, width), bf16),
            pltpu.VMEM((rows, width), bf16),
            pltpu.VMEM((rows, width), f32),
            pltpu.VMEM((2, width, width), f32),
            pltpu.VMEM((2, width, width), bf16),
            pltpu.VMEM((width, width), bf16),
            pltpu.VMEM((width, width), bf16),
            pltpu.VMEM((2, NX - 1, quarter, width), bf16),
            pltpu.VMEM((2, quarter, width), f32),
            pltpu.VMEM((2, quarter, width), bf16),
            pltpu.VMEM((2, NX - 1, part, width), bf16),
            pltpu.VMEM((NZ, 2, 8, wide), f32),
            pltpu.VMEM((NZ - 1, 2, 8, wide), f32),
            pltpu.VMEM((NZ, 2, 8, wide), f32),
            dma((STAGES, 2, NZ - 1)),
            dma((STAGES,)),
            dma((STAGES,)),
            dma((STAGES,)),
            dma((2, blocks)),
            dma((blocks,)),
            dma((NX, blocks)),
            dma,
            dma,
            dma((STAGES,)),
            dma((STAGES,)),
            dma((STAGES, 2, blocks)),
            dma((STAGES,)),
            dma,
            dma,
            dma,
            dma((2,)),
            dma,
            dma((2,)),
            dma,
            dma((2,)),
            dma,
            dma,
            dma,
            dma,
            dma,
            dma((2,)),
            dma,
            dma((2, NX - 1)),
            dma,
            dma((2, NX)),
        ],
        compiler_params=pltpu.CompilerParams(
            collective_id=0, has_side_effects=True, vmem_limit_bytes=56 * 2**20
        ),
        cost_estimate=pl.CostEstimate(
            flops=7 * 10**9, bytes_accessed=8 * 2**20, transcendentals=2**19
        ),
        name="layers",
    )(initial, history, tiles, cols, chosen, weight_one, weight_two, cotangent)


def finish_kernel(sum_ref, rows_ref, one_ref, two_ref, out_ref):
    one_ref[...] = BETA_ONE * sum_ref[0].astype(jnp.float32)
    two_ref[...] = BETA_TWO * sum_ref[1].astype(jnp.float32)
    out_ref[...] = rows_ref[...]


def finish(summed, output):
    width = summed.shape[1]
    rows = output.shape[0]
    steps = 4
    grad = pl.BlockSpec((width // steps, width), lambda n: (n, 0))
    out = pl.BlockSpec((rows // steps, width), lambda n: (n, 0))
    full = jax.ShapeDtypeStruct((width, width), jnp.float32)
    return pl.pallas_call(
        finish_kernel,
        grid=(steps,),
        out_shape=(full, full, jax.ShapeDtypeStruct(output.shape, output.dtype)),
        in_specs=[pl.BlockSpec((2, width // steps, width), lambda n: (0, n, 0)), out],
        out_specs=(grad, grad, out),
        compiler_params=pltpu.CompilerParams(vmem_limit_bytes=56 * 2**20),
        name="finish",
    )(summed, output)


def local(initial, history, tile_values, tile_cols, send_blocks, weight_one, weight_two, cotangent):
    tiles = tile_values[0]
    blocks, slots, size, _ = tiles.shape
    width = initial.shape[2]
    output, summed = layers(
        initial[0].reshape(blocks, size, width), history[0].reshape(blocks, size, width),
        tiles, tile_cols[0], send_blocks[0], weight_one, weight_two, cotangent[0],
    )
    grad_one, grad_two, output = finish(summed, output)
    return (output[None], grad_one, grad_two)


def solution(mesh):
    return jax.shard_map(
        local,
        mesh=mesh,
        in_specs=(
            P("grp", "dom", None),
            P("grp", "dom", None),
            P("grp", "dom", None, None, None),
            P("grp", "dom", None),
            P("grp", "dom", None),
            P(),
            P(),
            P("grp", "dom", None),
        ),
        out_specs=(P("grp", "dom", None), P(), P()),
        check_vma=False,
    )
```

```python
import functools

import jax
import jax.numpy as jnp
from jax import lax
from jax.experimental import pallas as pl
from jax.experimental.pallas import tpu as pltpu
from jax.sharding import PartitionSpec as P

RESTART = 0.1
BETA_ONE = 0.405465
BETA_TWO = 0.223144

NZ = 8
NX = 4
NY = 4
STAGES = 4
MESH = pl.DeviceIdType.MESH


def dom_index(z, x, core):
    return (z * NX + x) * 2 + core


def sigmoid(value):
    return 1.0 / (1.0 + jnp.exp(-value))


def dot(a, b, dims=((1,), (0,))):
    return lax.dot_general(a, b, (dims, ((), ())), preferred_element_type=jnp.float32)


def layers_kernel(
    initial_ref, history_ref, tiles_ref, cols_ref, chosen_ref, one_any, two_any, cot_any,
    out_ref, sum_ref, one_ref, two_ref, cot_ref, load_sem,
    feat0, feat1, feat2, feat3, tiles_all, part_out, part_in, relay_in, relay_sum, metas, metas_smem, table,
    local_ref, base_ref, received_ref, mixed_one_ref, mixed_two_ref, hidden_ref, slope_ref,
    grad_ref, send_ref, pair_in, pair_sum, first_in, first_sum, first_out, second_in,
    third, third_in, third_done,
    z_recv, sib_recv, z_send, own_sem, t_recv, t_far, t_sib, t_send, t_own, p_recv, p_send,
    relay_recv, relay_send, m_recv, m_send, m_copy, pair_send, pair_recv, first_send, first_recv,
    second_send, second_recv, third_send, third_recv, done_send, done_recv,
    gather_send, gather_recv, share_send, share_recv, back_send, back_recv,
):
    f32 = jnp.float32
    bf16 = jnp.bfloat16
    feats = (feat0, feat1, feat2, feat3)
    blocks, size, width = initial_ref.shape
    slots = tiles_ref.shape[1]
    wide = feat0.shape[2]
    rows = blocks * size
    dom = lax.axis_index("dom")
    my_y = lax.axis_index("grp")
    core = lax.rem(dom, 2)
    my_x = lax.rem(dom // 2, NX)
    my_z = dom // (2 * NX)
    other = 1 - core

    def at(dz, dx, flip, dy=0):
        z = lax.rem(my_z + dz, NZ)
        x = lax.rem(my_x + dx, NX)
        y = lax.rem(my_y + dy, NY)
        return (dom_index(z, x, other if flip else core), y)

    row = [(0, dx, f) for dx in range(NX) for f in range(2) if (dx, f) != (0, 0)]
    column = [(dz, 0, f) for dz in range(1, NZ) for f in range(2)]
    stack = [(0, 0, 0, dy) for dy in range(1, NY)]
    barrier = pltpu.get_barrier_semaphore()
    for peer in row + column + stack:
        pl.semaphore_signal(barrier, inc=1, device_id=at(*peer), device_id_type=MESH)
    pl.semaphore_wait(barrier, len(row) + len(column) + len(stack))

    def remote(src, dst, send_sem, recv_sem, peer):
        return pltpu.make_async_remote_copy(
            src_ref=src, dst_ref=dst, send_sem=send_sem, recv_sem=recv_sem,
            device_id=at(*peer), device_id_type=MESH,
        )

    def land(ref, sem):
        pltpu.make_async_copy(ref, ref, sem).wait()

    def feat_slot(stage, dz, flip):
        return feats[stage].at[pl.ds((dz * 2 + flip) * blocks, blocks)]

    def own_columns(stage, flip):
        ref = (initial_ref, history_ref)[stage // 2]
        half = other if flip else core
        start = pl.multiple_of((half * 2 + stage % 2) * wide, wide)
        return ref.at[:, :, pl.ds(start, wide)]

    def start_stage(stage):
        for flip in range(2):
            for direction, dz in ((0, 1), (1, NZ - 1)):
                remote(
                    own_columns(stage, flip), feat_slot(stage, NZ - dz, flip),
                    z_send.at[stage], z_recv.at[stage, direction, flip], (dz, 0, flip),
                ).start()
        remote(
            own_columns(stage, 1), feat_slot(stage, 0, 1),
            z_send.at[stage], sib_recv.at[stage], (0, 0, 1),
        ).start()
        pltpu.make_async_copy(own_columns(stage, 0), feat_slot(stage, 0, 0), own_sem.at[stage]).start()

    def ring_tick(stage, m):
        for direction, dz in ((0, 1), (1, NZ - 1)):
            hop = m // 2 + 1
            flip = m % 2 if hop < NZ // 2 else direction
            origin = (NZ - hop if direction == 0 else hop) % NZ
            slot = feat_slot(stage, origin, flip)
            land(slot, z_recv.at[stage, direction, m])
            if hop < NZ // 2 - 1 or (hop == NZ // 2 - 1 and flip == direction):
                later = m + 2 if hop < NZ // 2 - 1 else NZ - 2
                next_origin = (NZ - hop - 1 if direction == 0 else hop + 1) % NZ
                remote(
                    slot, feat_slot(stage, next_origin, flip),
                    z_send.at[stage], z_recv.at[stage, direction, later], (dz, 0, 0),
                ).start()

    def tile_slot(dx, flip, i):
        return tiles_all.at[dx * 2 + flip, i]

    def send_tiles(which):
        for n in which:
            for i, dx, sem in ((n, 1, 0), (blocks - 1 - n, NX - 1, 1)):
                remote(
                    tiles_ref.at[i], tile_slot(NX - dx, 0, i), t_send, t_recv.at[sem, i], (0, dx, 0)
                ).start()

    def share_tiles(dx, i):
        remote(
            tile_slot(dx, 0, i), tile_slot(dx, 1, i), t_send, t_sib.at[dx, i], (0, 0, 1)
        ).start()

    def pass_tiles(which):
        for n in which:
            for i, dx, sem in ((n, NX - 1, 0), (blocks - 1 - n, 1, 1)):
                land(tile_slot(dx, 0, i), t_recv.at[sem, i])
                if n < blocks // 2:
                    toward = 1 if sem == 0 else NX - 1
                    remote(
                        tile_slot(dx, 0, i), tile_slot(2, 0, i), t_send, t_far.at[i], (0, toward, 0)
                    ).start()
                share_tiles(dx, i)

    near = [(0, 0, 1)] + [p for p in row if p[1] != 0] + column
    metas[0, pl.ds(0, blocks), pl.ds(0, slots)] = cols_ref[...]
    metas[0, pl.ds(blocks, 1), pl.ds(0, chosen_ref.shape[1])] = chosen_ref[...]
    start_stage(0)
    for peer in near:
        dz, dx, f = peer
        if dz == 0:
            slot = ((NX - dx) % NX) * 2 + f
        else:
            slot = 2 * NX + (NZ - dz - 1) * 2 + f
        remote(metas.at[0], metas.at[slot], m_send, m_recv, peer).start()
    for i in range(blocks):
        remote(tiles_ref.at[i], tile_slot(0, 1, i), t_send, t_sib.at[0, i], (0, 0, 1)).start()
    loads = [
        pltpu.make_async_copy(src, dst, load_sem.at[n])
        for n, (src, dst) in enumerate(((one_any, one_ref), (two_any, two_ref), (cot_any, cot_ref)))
    ]
    for load in loads:
        load.start()
    send_tiles(range(blocks // 2))
    own_tiles = pltpu.make_async_copy(tiles_ref, tiles_all.at[0], t_own)
    own_tiles.start()
    for f in feats:
        f[2 * NZ * blocks] = jnp.zeros((size, wide), f.dtype)

    def copy_metas():
        land(metas.at[pl.ds(1, len(near))], m_recv)
        copy = pltpu.make_async_copy(metas, metas_smem, m_copy)
        copy.start()
        copy.wait()

    def build_table(readers):
        for reader in readers:
            dx, f = reader // 2, reader % 2
            reader_index = dom_index(my_z, lax.rem(my_x + dx, NX), other if f else core)

            def entry(n, carry):
                col = metas_smem[reader, lax.div(n, slots), lax.rem(n, slots)]
                owner = jnp.maximum(col - blocks, 0)
                chip = lax.div(owner, 2)
                valid = (col >= blocks) & (lax.rem(chip, NX) == my_x)
                dz = lax.rem(lax.div(chip, NX) + (NZ - my_z), NZ)
                flip = lax.rem(owner + core, 2)
                place = dz * 2 + flip
                where = jnp.where(dz == 0, flip, place + (2 * NX - 2))
                block = metas_smem[where, blocks, reader_index]
                slot = place * blocks + block
                table[reader * blocks * slots + n] = jnp.where(valid, slot, 2 * NZ * blocks)
                return carry

            lax.fori_loop(0, blocks * slots, entry, 0, unroll=slots)

    def build_local(i):
        sums = [jnp.zeros((size, size), f32) for _ in range(blocks)]
        for k in range(slots):
            tile = tiles_ref[i, k].astype(f32)
            for c in range(blocks):
                mask = jnp.where(metas_smem[0, i, k] == c, 1.0, 0.0).astype(f32)
                sums[c] += tile * mask
        for c in range(blocks):
            local_ref[pl.ds(i * size, size), pl.ds(c * size, size)] = sums[c].astype(bf16)

    def product(stage, reader, i):
        first = (reader * blocks + i) * slots
        left = jnp.concatenate([tiles_all[reader, i, k] for k in range(slots)], axis=1)
        right = jnp.concatenate([feats[stage][table[first + k]] for k in range(slots)], axis=0)
        return dot(left, right)

    def send_part(stage, reader, which=slice(None)):
        dx, f = reader // 2, reader % 2
        if dx == 2:
            toward = 1 if f == 0 else NX - 1
            remote(
                part_out.at[stage, reader, which], relay_in.at[stage, f, which],
                relay_send.at[stage], relay_recv.at[stage, f, 0 if which == slice(None) else which],
                (0, toward, 0),
            ).start()
        elif reader:
            source = {0: 0, 1: 2, NX - 1: 1}[dx]
            remote(
                part_out.at[stage, reader, which], part_in.at[stage, source * 2 + f, which],
                p_send.at[stage], p_recv.at[stage], (0, dx, f),
            ).start()

    def partial(stage, reader):
        dx, f = reader // 2, reader % 2
        relays = (dx, f) in ((1, 0), (NX - 1, 1))
        if relays:
            land(relay_in.at[stage, f], relay_recv.at[stage, f, 0])

        def one(i, carry):
            total = product(stage, reader, i)
            if relays:
                total += relay_in[stage, f, i].astype(f32)
            part_out[stage, reader, i] = total.astype(bf16)
            return carry

        lax.fori_loop(0, blocks, one, 0, unroll=blocks)
        send_part(stage, reader)

    def last_partials():
        stage = STAGES - 1
        for reader in (4, 5, 3, 6):
            totals = [product(stage, reader, i) for i in range(blocks)]
            for i in range(blocks):
                part_out[stage, reader, i] = totals[i].astype(bf16)
            if reader // 2 == 2:
                for i in range(blocks):
                    send_part(stage, reader, i)
            else:
                send_part(stage, reader)
        relayed = (2, 7)
        for reader in relayed:
            for i in range(blocks):
                relay_sum[reader % 2, i] = product(stage, reader, i)
        for i in range(blocks):
            for reader in relayed:
                f = reader % 2
                land(relay_in.at[stage, f, i], relay_recv.at[stage, f, i])
                total = relay_sum[f, i] + relay_in[stage, f, i].astype(f32)
                part_out[stage, reader, i] = total.astype(bf16)
                send_part(stage, reader, i)
        for reader in (1, 0):
            for i in range(blocks):
                part_out[stage, reader, i] = product(stage, reader, i).astype(bf16)
            send_part(stage, reader)

    def column_chunk(stage, flip):
        return (other if flip else core) * 2 + stage % 2

    def total_of(stage, flip):
        first = part_in[stage, 1] if flip else part_out[stage, 0]
        total = first.astype(f32)
        for source in (1, 2):
            total += part_in[stage, source * 2 + flip].astype(f32)
        return total.reshape(rows, wide)

    def received(stage):
        land(part_in.at[stage, pl.ds(1, 5)], p_recv.at[stage])

    def finish_one(stage):
        received(stage)
        for flip in range(2):
            received_ref[column_chunk(stage, flip)] = total_of(stage, flip)

    def layer_one(i):
        here = pl.ds(i * size, size)
        local = local_ref[here, :]
        own = initial_ref[...].reshape(rows, width)
        got = jnp.concatenate([received_ref[q, here, :] for q in range(4)], axis=1)
        mixed = (
            (1.0 - RESTART) * (dot(local, own) + got) + RESTART * initial_ref[i].astype(f32)
        ).astype(bf16)
        pre = (1.0 - BETA_ONE) * mixed.astype(f32) + BETA_ONE * dot(mixed, one_ref[...])
        sig = sigmoid(pre)
        mixed_one_ref[here, :] = mixed
        hidden_ref[here, :] = (pre * sig).astype(bf16)
        slope_ref[here, :] = sig * (1.0 + pre * (1.0 - sig))

    def start_two():
        total = (1.0 - RESTART) * dot(local_ref[...], hidden_ref[...]) + RESTART * initial_ref[
            ...
        ].reshape(rows, width).astype(f32)
        for q in range(4):
            base_ref[q] = total[:, q * wide : (q + 1) * wide]

    def finish_two(stage):
        received(stage)
        for flip in range(2):
            chunk = column_chunk(stage, flip)
            mixed = base_ref[chunk] + (1.0 - RESTART) * total_of(stage, flip)
            mixed_two_ref[:, pl.ds(pl.multiple_of(chunk * wide, wide), wide)] = mixed.astype(bf16)

    def store_grad(g, grad):
        grad_ref[g] = grad
        send_ref[g] = grad.astype(bf16)

    def layer_two():
        mixed_two = mixed_two_ref[...]
        pre_two = (1.0 - BETA_TWO) * mixed_two.astype(f32) + BETA_TWO * dot(mixed_two, two_ref[...])
        sig = sigmoid(pre_two)
        out_ref[...] = (pre_two * sig).astype(bf16)
        slope_two = sig * (1.0 + pre_two * (1.0 - sig))
        back_two = (cot_ref[...].astype(f32) * slope_two).astype(bf16)
        back_mixed = (
            (1.0 - BETA_TWO) * back_two.astype(f32)
            + BETA_TWO * dot(back_two, two_ref[...], ((1,), (1,)))
        ).astype(bf16)
        back_hidden = (1.0 - RESTART) * dot(local_ref[...], back_mixed, ((0,), (0,)))
        back_one = (back_hidden * slope_ref[...]).astype(bf16)
        store_grad(1, dot(mixed_two, back_two, ((0,), (0,))))
        store_grad(0, dot(mixed_one_ref[...], back_one, ((0,), (0,))))

    turns = {(stage, m): [] for stage in range(STAGES) for m in range(NZ - 1)}
    for m, dx, f in ((0, 0, 1), (1, 0, 0), (2, 1, 1), (3, 3, 0), (5, 2, 0), (6, 2, 1)):
        turns[1, m].append((0, dx, f))
    turns[2, 2].append((0, 1, 0))
    turns[2, 3].append((0, 3, 1))
    order = [(2, 0), (2, 1), (1, 1), (3, 0), (1, 0), (3, 1), (0, 1), (0, 0)]
    for stage in range(2, STAGES):
        for turn, (dx, f) in enumerate(order):
            turns[stage, min(turn, NZ - 2)].append((stage - 1, dx, f))

    for stage in range(STAGES):
        for m in range(NZ - 1):
            ring_tick(stage, m)
            if m == 5 and stage + 1 < STAGES:
                start_stage(stage + 1)
            if stage == 0:
                if m == 1:
                    send_tiles(range(blocks // 2, blocks))
                    copy_metas()
                if m in (2, 3, 4, 6):
                    build_table({2: (1, 0), 3: (3, 6), 4: (4, 5), 6: (2, 7)}[m])
                if m == 5:
                    pass_tiles(range(blocks // 2))
                continue
            if stage == 1:
                if m == 0:
                    for load in loads:
                        load.wait()
                    own_tiles.wait()
                    for i in range(blocks):
                        land(tile_slot(0, 1, i), t_sib.at[0, i])
                if m == 1:
                    pass_tiles(range(blocks // 2, blocks))
                if m == 2:
                    for i in range(blocks):
                        land(tile_slot(1, 1, i), t_sib.at[1, i])
                        land(tile_slot(NX - 1, 1, i), t_sib.at[NX - 1, i])
                if m == 5:
                    for i in range(blocks):
                        land(tile_slot(2, 0, i), t_far.at[i])
                        share_tiles(2, i)
                if m == 6:
                    for i in range(blocks):
                        land(tile_slot(2, 1, i), t_sib.at[2, i])
            for of, dx, f in turns[stage, m]:
                partial(of, dx * 2 + f)
        land(feat_slot(stage, 0, 1), sib_recv.at[stage])
        land(feat_slot(stage, 0, 0), own_sem.at[stage])
    last_partials()
    for stage in range(2):
        finish_one(stage)
    for i in range(blocks):
        build_local(i)
        layer_one(i)
    start_two()
    finish_two(2)
    finish_two(3)
    layer_two()

    half = width // 2
    quarter = half // NX
    part = quarter // NX
    place = ((my_x, my_y), (my_y, my_x))

    def rows_at(start, count):
        return pl.ds(pl.multiple_of(start, part), count)

    def along(h, turn, d):
        return (0, d, 0) if h == turn else (0, 0, 0, d)

    for h in range(2):
        here = pl.ds(h * half, half)
        remote(
            send_ref.at[other, here], pair_in.at[here], pair_send, pair_recv.at[h], (0, 0, 1)
        ).start()
    for h in range(2):
        here = pl.ds(h * half, half)
        land(pair_in.at[here], pair_recv.at[h])
        pair_sum[here, :] = (grad_ref[core, here, :] + pair_in[here, :].astype(f32)).astype(bf16)
        for d in (2, 1, 3):
            theirs = rows_at(h * half + lax.rem(place[h][0] + d, NX) * quarter, quarter)
            remote(
                pair_sum.at[theirs], first_in.at[h, NX - d - 1],
                first_send, first_recv.at[h], along(h, 0, d),
            ).start()
    for h in range(2):
        mine = rows_at(h * half + place[h][0] * quarter, quarter)
        value = grad_ref[core, mine, :] + pair_in[mine, :].astype(f32)
        land(first_in.at[h], first_recv.at[h])
        for n in range(NX - 1):
            value += first_in[h, n].astype(f32)
        first_sum[h] = value
        first_out[h] = value.astype(bf16)
        for d in (2, 1, 3):
            theirs = rows_at(lax.rem(place[h][1] + d, NX) * part, part)
            remote(
                first_out.at[h, theirs], second_in.at[h, NX - d - 1],
                second_send, second_recv.at[h], along(h, 1, d),
            ).start()
    tiles_of = [(r, q) for r in range(part // 8) for q in range(4)]
    for h in range(2):
        value = first_sum[h, rows_at(place[h][1] * part, part), :]
        land(second_in.at[h], second_recv.at[h])
        for n in range(NX - 1):
            value += second_in[h, n].astype(f32)
        for n, (r, q) in enumerate(tiles_of):
            third[n, h] = value[r * 8 : (r + 1) * 8, q * wide : (q + 1) * wide]
    for dz in (4, 3, 5, 2, 6, 1, 7):
        remote(
            third.at[lax.rem(my_z + dz, NZ)], third_in.at[NZ - dz - 1],
            third_send, third_recv, (dz, 0, 0),
        ).start()
    value = third[my_z]
    land(third_in, third_recv)
    for n in range(NZ - 1):
        value += third_in[n]
    third_done[my_z] = value
    for dz in (4, 3, 5, 2, 6, 1, 7):
        remote(
            third_done.at[my_z], third_done.at[my_z], done_send, done_recv, (dz, 0, 0)
        ).start()
    land(third_done.at[pl.ds(0, NZ - 1)], done_recv)

    for h in range(2):
        value = jnp.concatenate(
            [
                jnp.concatenate([third_done[r * 4 + q, h] for q in range(4)], axis=1)
                for r in range(part // 8)
            ],
            axis=0,
        )
        mine = rows_at(h * half + place[h][0] * quarter + place[h][1] * part, part)
        sum_ref[core, mine, :] = value.astype(bf16)
        for d in (2, 1, 3):
            remote(
                sum_ref.at[core, mine], sum_ref.at[core, mine],
                gather_send, gather_recv.at[h], along(h, 1, d),
            ).start()
    for h in range(2):
        land(second_in.at[h], gather_recv.at[h])
        mine = rows_at(h * half + place[h][0] * quarter, quarter)
        for d in (2, 1, 3):
            remote(
                sum_ref.at[core, mine], sum_ref.at[core, mine],
                share_send, share_recv.at[h, NX - d - 1], along(h, 0, d),
            ).start()
        remote(
            sum_ref.at[core, mine], sum_ref.at[core, mine],
            back_send, back_recv.at[h, 0], (0, 0, 1),
        ).start()

    def share_at(h, d):
        return rows_at(h * half + lax.rem(place[h][0] + d, NX) * quarter, quarter)

    for d in (1, 3, 2):
        for h in range(2):
            got = share_at(h, d)
            land(sum_ref.at[core, got], share_recv.at[h, d - 1])
            remote(
                sum_ref.at[core, got], sum_ref.at[core, got],
                back_send, back_recv.at[h, d], (0, 0, 1),
            ).start()
    for d in range(NX):
        for h in range(2):
            land(sum_ref.at[other, share_at(h, d)], back_recv.at[h, d])

    for stage in range(STAGES):
        land(feats[stage].at[pl.ds(0, 15 * blocks)], z_send.at[stage])
        land(part_in.at[stage, pl.ds(1, 5)], p_send.at[stage])
        land(relay_in.at[stage], relay_send.at[stage])
    land(metas.at[pl.ds(1, len(near))], m_send)
    land(tiles_all.at[pl.ds(1, 2 * NX - 1)], t_send)
    land(pair_in, pair_send)
    land(first_in, first_send)
    land(second_in, second_send)
    land(third_in, third_send)
    land(third_in, done_send)
    land(second_in, gather_send)
    land(first_in, share_send)
    land(pair_in, back_send)


def layers(initial, history, tiles, cols, chosen, weight_one, weight_two, cotangent):
    blocks, size, width = initial.shape
    slots = tiles.shape[1]
    wide = width // 4
    rows = blocks * size
    quarter = width // 2 // NX
    part = quarter // NX
    vmem = pl.BlockSpec(memory_space=pltpu.VMEM)
    dma = pltpu.SemaphoreType.DMA
    bf16 = jnp.bfloat16
    f32 = jnp.float32
    metas = 2 * NX + 2 * (NZ - 1)
    return pl.pallas_call(
        layers_kernel,
        out_shape=(
            jax.ShapeDtypeStruct((rows, width), bf16),
            jax.ShapeDtypeStruct((2, width, width), bf16),
        ),
        in_specs=[vmem] * 5 + [pl.BlockSpec(memory_space=pl.ANY)] * 3,
        out_specs=(vmem, vmem),
        scratch_shapes=[pltpu.VMEM((width, width), bf16)] * 2
        + [pltpu.VMEM((rows, width), bf16), dma((3,))]
        + [pltpu.VMEM((2 * NZ * blocks + 1, size, wide), bf16)] * STAGES
        + [
            pltpu.VMEM((2 * NX, blocks, slots, size, size), bf16),
            pltpu.VMEM((STAGES, 2 * NX, blocks, size, wide), bf16),
            pltpu.VMEM((STAGES, 6, blocks, size, wide), bf16),
            pltpu.VMEM((STAGES, 2, blocks, size, wide), bf16),
            pltpu.VMEM((2, blocks, size, wide), f32),
            pltpu.VMEM((metas, 8, 128), jnp.int32),
            pltpu.SMEM((metas, 8, 128), jnp.int32),
            pltpu.SMEM((2 * NX * blocks * slots,), jnp.int32),
            pltpu.VMEM((rows, rows), bf16),
            pltpu.VMEM((4, rows, wide), f32),
            pltpu.VMEM((4, rows, wide), f32),
            pltpu.VMEM((rows, width), bf16),
            pltpu.VMEM((rows, width), bf16),
            pltpu.VMEM((rows, width), bf16),
            pltpu.VMEM((rows, width), f32),
            pltpu.VMEM((2, width, width), f32),
            pltpu.VMEM((2, width, width), bf16),
            pltpu.VMEM((width, width), bf16),
            pltpu.VMEM((width, width), bf16),
            pltpu.VMEM((2, NX - 1, quarter, width), bf16),
            pltpu.VMEM((2, quarter, width), f32),
            pltpu.VMEM((2, quarter, width), bf16),
            pltpu.VMEM((2, NX - 1, part, width), bf16),
            pltpu.VMEM((NZ, 2, 8, wide), f32),
            pltpu.VMEM((NZ - 1, 2, 8, wide), f32),
            pltpu.VMEM((NZ, 2, 8, wide), f32),
            dma((STAGES, 2, NZ - 1)),
            dma((STAGES,)),
            dma((STAGES,)),
            dma((STAGES,)),
            dma((2, blocks)),
            dma((blocks,)),
            dma((NX, blocks)),
            dma,
            dma,
            dma((STAGES,)),
            dma((STAGES,)),
            dma((STAGES, 2, blocks)),
            dma((STAGES,)),
            dma,
            dma,
            dma,
            dma,
            dma((2,)),
            dma,
            dma((2,)),
            dma,
            dma((2,)),
            dma,
            dma,
            dma,
            dma,
            dma,
            dma((2,)),
            dma,
            dma((2, NX - 1)),
            dma,
            dma((2, NX)),
        ],
        compiler_params=pltpu.CompilerParams(
            collective_id=0, has_side_effects=True, vmem_limit_bytes=56 * 2**20
        ),
        cost_estimate=pl.CostEstimate(
            flops=7 * 10**9, bytes_accessed=8 * 2**20, transcendentals=2**19
        ),
        name="layers",
    )(initial, history, tiles, cols, chosen, weight_one, weight_two, cotangent)


def finish_kernel(sum_ref, rows_ref, one_ref, two_ref, out_ref):
    one_ref[...] = BETA_ONE * sum_ref[0].astype(jnp.float32)
    two_ref[...] = BETA_TWO * sum_ref[1].astype(jnp.float32)
    out_ref[...] = rows_ref[...]


def finish(summed, output):
    width = summed.shape[1]
    rows = output.shape[0]
    steps = 2
    grad = pl.BlockSpec((width // steps, width), lambda n: (n, 0))
    out = pl.BlockSpec((rows // steps, width), lambda n: (n, 0))
    full = jax.ShapeDtypeStruct((width, width), jnp.float32)
    return pl.pallas_call(
        finish_kernel,
        grid=(steps,),
        out_shape=(full, full, jax.ShapeDtypeStruct(output.shape, output.dtype)),
        in_specs=[pl.BlockSpec((2, width // steps, width), lambda n: (0, n, 0)), out],
        out_specs=(grad, grad, out),
        compiler_params=pltpu.CompilerParams(vmem_limit_bytes=56 * 2**20),
        name="finish",
    )(summed, output)


def local(initial, history, tile_values, tile_cols, send_blocks, weight_one, weight_two, cotangent):
    tiles = tile_values[0]
    blocks, slots, size, _ = tiles.shape
    width = initial.shape[2]
    output, summed = layers(
        initial[0].reshape(blocks, size, width), history[0].reshape(blocks, size, width),
        tiles, tile_cols[0], send_blocks[0], weight_one, weight_two, cotangent[0],
    )
    grad_one, grad_two, output = finish(summed, output)
    return (output[None], grad_one, grad_two)


def solution(mesh):
    return jax.shard_map(
        local,
        mesh=mesh,
        in_specs=(
            P("grp", "dom", None),
            P("grp", "dom", None),
            P("grp", "dom", None, None, None),
            P("grp", "dom", None),
            P("grp", "dom", None),
            P(),
            P(),
            P("grp", "dom", None),
        ),
        out_specs=(P("grp", "dom", None), P(), P()),
        check_vma=False,
    )
```

```python
import functools

import jax
import jax.numpy as jnp
from jax import lax
from jax.experimental import pallas as pl
from jax.experimental.pallas import tpu as pltpu
from jax.sharding import PartitionSpec as P

RESTART = 0.1
BETA_ONE = 0.405465
BETA_TWO = 0.223144

NZ = 8
NX = 4
NY = 4
STAGES = 4
MESH = pl.DeviceIdType.MESH


def dom_index(z, x, core):
    return (z * NX + x) * 2 + core


def sigmoid(value):
    return 1.0 / (1.0 + jnp.exp(-value))


def dot(a, b, dims=((1,), (0,))):
    return lax.dot_general(a, b, (dims, ((), ())), preferred_element_type=jnp.float32)


def layers_kernel(
    initial_ref, history_ref, tiles_ref, cols_ref, chosen_ref, one_any, two_any, cot_any,
    out_ref, sum_ref, one_ref, two_ref, cot_ref, load_sem,
    feat0, feat1, feat2, feat3, tiles_all, part_out, part_in, relay_in, relay_sum, metas, metas_smem, table,
    local_ref, base_ref, received_ref, mixed_one_ref, mixed_two_ref, hidden_ref, slope_ref,
    grad_ref, send_ref, pair_in, pair_sum, first_in, first_sum, first_out, second_in,
    third, third_in, third_done,
    z_recv, sib_recv, z_send, own_sem, t_recv, t_far, t_sib, t_send, t_own, p_recv, p_send,
    relay_recv, relay_send, m_recv, m_send, m_copy, pair_send, pair_recv, first_send, first_recv,
    second_send, second_recv, third_send, third_recv, done_send, done_recv,
    gather_send, gather_recv, share_send, share_recv, back_send, back_recv,
):
    f32 = jnp.float32
    bf16 = jnp.bfloat16
    feats = (feat0, feat1, feat2, feat3)
    blocks, size, width = initial_ref.shape
    slots = tiles_ref.shape[1]
    wide = feat0.shape[2]
    rows = blocks * size
    dom = lax.axis_index("dom")
    my_y = lax.axis_index("grp")
    core = lax.rem(dom, 2)
    my_x = lax.rem(dom // 2, NX)
    my_z = dom // (2 * NX)
    other = 1 - core

    def at(dz, dx, flip, dy=0):
        z = lax.rem(my_z + dz, NZ)
        x = lax.rem(my_x + dx, NX)
        y = lax.rem(my_y + dy, NY)
        return (dom_index(z, x, other if flip else core), y)

    row = [(0, dx, f) for dx in range(NX) for f in range(2) if (dx, f) != (0, 0)]
    column = [(dz, 0, f) for dz in range(1, NZ) for f in range(2)]
    stack = [(0, 0, 0, dy) for dy in range(1, NY)]
    barrier = pltpu.get_barrier_semaphore()
    for peer in row + column + stack:
        pl.semaphore_signal(barrier, inc=1, device_id=at(*peer), device_id_type=MESH)
    pl.semaphore_wait(barrier, len(row) + len(column) + len(stack))

    def remote(src, dst, send_sem, recv_sem, peer):
        return pltpu.make_async_remote_copy(
            src_ref=src, dst_ref=dst, send_sem=send_sem, recv_sem=recv_sem,
            device_id=at(*peer), device_id_type=MESH,
        )

    def land(ref, sem):
        pltpu.make_async_copy(ref, ref, sem).wait()

    def feat_slot(stage, dz, flip):
        return feats[stage].at[pl.ds((dz * 2 + flip) * blocks, blocks)]

    def own_columns(stage, flip):
        ref = (initial_ref, history_ref)[stage // 2]
        half = other if flip else core
        start = pl.multiple_of((half * 2 + stage % 2) * wide, wide)
        return ref.at[:, :, pl.ds(start, wide)]

    def start_stage(stage):
        for flip in range(2):
            for direction, dz in ((0, 1), (1, NZ - 1)):
                remote(
                    own_columns(stage, flip), feat_slot(stage, NZ - dz, flip),
                    z_send.at[stage], z_recv.at[stage, direction, flip], (dz, 0, flip),
                ).start()
        remote(
            own_columns(stage, 1), feat_slot(stage, 0, 1),
            z_send.at[stage], sib_recv.at[stage], (0, 0, 1),
        ).start()
        pltpu.make_async_copy(own_columns(stage, 0), feat_slot(stage, 0, 0), own_sem.at[stage]).start()

    def ring_tick(stage, m):
        for direction, dz in ((0, 1), (1, NZ - 1)):
            hop = m // 2 + 1
            flip = m % 2 if hop < NZ // 2 else direction
            origin = (NZ - hop if direction == 0 else hop) % NZ
            slot = feat_slot(stage, origin, flip)
            land(slot, z_recv.at[stage, direction, m])
            if hop < NZ // 2 - 1 or (hop == NZ // 2 - 1 and flip == direction):
                later = m + 2 if hop < NZ // 2 - 1 else NZ - 2
                next_origin = (NZ - hop - 1 if direction == 0 else hop + 1) % NZ
                remote(
                    slot, feat_slot(stage, next_origin, flip),
                    z_send.at[stage], z_recv.at[stage, direction, later], (dz, 0, 0),
                ).start()

    def tile_slot(dx, flip, i):
        return tiles_all.at[dx * 2 + flip, i]

    def send_tiles(which):
        for n in which:
            for i, dx, sem in ((n, 1, 0), (blocks - 1 - n, NX - 1, 1)):
                remote(
                    tiles_ref.at[i], tile_slot(NX - dx, 0, i), t_send, t_recv.at[sem, i], (0, dx, 0)
                ).start()

    def share_tiles(dx, i):
        remote(
            tile_slot(dx, 0, i), tile_slot(dx, 1, i), t_send, t_sib.at[dx, i], (0, 0, 1)
        ).start()

    def pass_tiles(which):
        for n in which:
            for i, dx, sem in ((n, NX - 1, 0), (blocks - 1 - n, 1, 1)):
                land(tile_slot(dx, 0, i), t_recv.at[sem, i])
                if n < blocks // 2:
                    toward = 1 if sem == 0 else NX - 1
                    remote(
                        tile_slot(dx, 0, i), tile_slot(2, 0, i), t_send, t_far.at[i], (0, toward, 0)
                    ).start()
                share_tiles(dx, i)

    near = [(0, 0, 1)] + [p for p in row if p[1] != 0] + column
    metas[0, pl.ds(0, blocks), pl.ds(0, slots)] = cols_ref[...]
    metas[0, pl.ds(blocks, 1), pl.ds(0, chosen_ref.shape[1])] = chosen_ref[...]
    start_stage(0)
    for peer in near:
        dz, dx, f = peer
        if dz == 0:
            slot = ((NX - dx) % NX) * 2 + f
        else:
            slot = 2 * NX + (NZ - dz - 1) * 2 + f
        remote(metas.at[0], metas.at[slot], m_send, m_recv, peer).start()
    for i in range(blocks):
        remote(tiles_ref.at[i], tile_slot(0, 1, i), t_send, t_sib.at[0, i], (0, 0, 1)).start()
    loads = [
        pltpu.make_async_copy(src, dst, load_sem.at[n])
        for n, (src, dst) in enumerate(((one_any, one_ref), (two_any, two_ref), (cot_any, cot_ref)))
    ]
    for load in loads:
        load.start()
    send_tiles(range(blocks // 2))
    own_tiles = pltpu.make_async_copy(tiles_ref, tiles_all.at[0], t_own)
    own_tiles.start()
    for f in feats:
        f[2 * NZ * blocks] = jnp.zeros((size, wide), f.dtype)

    def copy_metas():
        land(metas.at[pl.ds(1, len(near))], m_recv)
        copy = pltpu.make_async_copy(metas, metas_smem, m_copy)
        copy.start()
        copy.wait()

    def build_table(readers):
        for reader in readers:
            dx, f = reader // 2, reader % 2
            reader_index = dom_index(my_z, lax.rem(my_x + dx, NX), other if f else core)

            def entry(n, carry):
                col = metas_smem[reader, lax.div(n, slots), lax.rem(n, slots)]
                owner = jnp.maximum(col - blocks, 0)
                chip = lax.div(owner, 2)
                valid = (col >= blocks) & (lax.rem(chip, NX) == my_x)
                dz = lax.rem(lax.div(chip, NX) + (NZ - my_z), NZ)
                flip = lax.rem(owner + core, 2)
                place = dz * 2 + flip
                where = jnp.where(dz == 0, flip, place + (2 * NX - 2))
                block = metas_smem[where, blocks, reader_index]
                slot = place * blocks + block
                table[reader * blocks * slots + n] = jnp.where(valid, slot, 2 * NZ * blocks)
                return carry

            lax.fori_loop(0, blocks * slots, entry, 0, unroll=slots)

    def build_local(i):
        sums = [jnp.zeros((size, size), f32) for _ in range(blocks)]
        for k in range(slots):
            tile = tiles_ref[i, k].astype(f32)
            for c in range(blocks):
                mask = jnp.where(metas_smem[0, i, k] == c, 1.0, 0.0).astype(f32)
                sums[c] += tile * mask
        for c in range(blocks):
            local_ref[pl.ds(i * size, size), pl.ds(c * size, size)] = sums[c].astype(bf16)

    def product(stage, reader, i):
        first = (reader * blocks + i) * slots
        left = jnp.concatenate([tiles_all[reader, i, k] for k in range(slots)], axis=1)
        right = jnp.concatenate([feats[stage][table[first + k]] for k in range(slots)], axis=0)
        return dot(left, right)

    def send_part(stage, reader, which=slice(None)):
        dx, f = reader // 2, reader % 2
        if dx == 2:
            toward = 1 if f == 0 else NX - 1
            remote(
                part_out.at[stage, reader, which], relay_in.at[stage, f, which],
                relay_send.at[stage], relay_recv.at[stage, f, 0 if which == slice(None) else which],
                (0, toward, 0),
            ).start()
        elif reader:
            source = {0: 0, 1: 2, NX - 1: 1}[dx]
            remote(
                part_out.at[stage, reader, which], part_in.at[stage, source * 2 + f, which],
                p_send.at[stage], p_recv.at[stage], (0, dx, f),
            ).start()

    def partial(stage, reader):
        dx, f = reader // 2, reader % 2
        relays = (dx, f) in ((1, 0), (NX - 1, 1))
        if relays:
            land(relay_in.at[stage, f], relay_recv.at[stage, f, 0])

        def one(i, carry):
            total = product(stage, reader, i)
            if relays:
                total += relay_in[stage, f, i].astype(f32)
            part_out[stage, reader, i] = total.astype(bf16)
            return carry

        lax.fori_loop(0, blocks, one, 0, unroll=blocks)
        send_part(stage, reader)

    def last_partials():
        stage = STAGES - 1
        for reader in (4, 5, 3, 6):
            totals = [product(stage, reader, i) for i in range(blocks)]
            for i in range(blocks):
                part_out[stage, reader, i] = totals[i].astype(bf16)
            if reader // 2 == 2:
                for i in range(blocks):
                    send_part(stage, reader, i)
            else:
                send_part(stage, reader)
        relayed = (2, 7)
        for reader in relayed:
            for i in range(blocks):
                relay_sum[reader % 2, i] = product(stage, reader, i)
        for i in range(blocks):
            for reader in relayed:
                f = reader % 2
                land(relay_in.at[stage, f, i], relay_recv.at[stage, f, i])
                total = relay_sum[f, i] + relay_in[stage, f, i].astype(f32)
                part_out[stage, reader, i] = total.astype(bf16)
                send_part(stage, reader, i)
        for reader in (1, 0):
            for i in range(blocks):
                part_out[stage, reader, i] = product(stage, reader, i).astype(bf16)
            send_part(stage, reader)

    def column_chunk(stage, flip):
        return (other if flip else core) * 2 + stage % 2

    def total_of(stage, flip):
        first = part_in[stage, 1] if flip else part_out[stage, 0]
        total = first.astype(f32)
        for source in (1, 2):
            total += part_in[stage, source * 2 + flip].astype(f32)
        return total.reshape(rows, wide)

    def received(stage):
        land(part_in.at[stage, pl.ds(1, 5)], p_recv.at[stage])

    def finish_one(stage):
        received(stage)
        for flip in range(2):
            received_ref[column_chunk(stage, flip)] = total_of(stage, flip)

    def layer_one(i):
        here = pl.ds(i * size, size)
        local = local_ref[here, :]
        own = initial_ref[...].reshape(rows, width)
        got = jnp.concatenate([received_ref[q, here, :] for q in range(4)], axis=1)
        mixed = (
            (1.0 - RESTART) * (dot(local, own) + got) + RESTART * initial_ref[i].astype(f32)
        ).astype(bf16)
        pre = (1.0 - BETA_ONE) * mixed.astype(f32) + BETA_ONE * dot(mixed, one_ref[...])
        sig = sigmoid(pre)
        mixed_one_ref[here, :] = mixed
        hidden_ref[here, :] = (pre * sig).astype(bf16)
        slope_ref[here, :] = sig * (1.0 + pre * (1.0 - sig))

    def start_two():
        total = (1.0 - RESTART) * dot(local_ref[...], hidden_ref[...]) + RESTART * initial_ref[
            ...
        ].reshape(rows, width).astype(f32)
        for q in range(4):
            base_ref[q] = total[:, q * wide : (q + 1) * wide]

    def finish_two(stage):
        received(stage)
        for flip in range(2):
            chunk = column_chunk(stage, flip)
            mixed = base_ref[chunk] + (1.0 - RESTART) * total_of(stage, flip)
            mixed_two_ref[:, pl.ds(pl.multiple_of(chunk * wide, wide), wide)] = mixed.astype(bf16)

    def store_grad(g, grad):
        grad_ref[g] = grad
        send_ref[g] = grad.astype(bf16)

    def layer_two():
        mixed_two = mixed_two_ref[...]
        pre_two = (1.0 - BETA_TWO) * mixed_two.astype(f32) + BETA_TWO * dot(mixed_two, two_ref[...])
        sig = sigmoid(pre_two)
        out_ref[...] = (pre_two * sig).astype(bf16)
        slope_two = sig * (1.0 + pre_two * (1.0 - sig))
        back_two = (cot_ref[...].astype(f32) * slope_two).astype(bf16)
        back_mixed = (
            (1.0 - BETA_TWO) * back_two.astype(f32)
            + BETA_TWO * dot(back_two, two_ref[...], ((1,), (1,)))
        ).astype(bf16)
        back_hidden = (1.0 - RESTART) * dot(local_ref[...], back_mixed, ((0,), (0,)))
        back_one = (back_hidden * slope_ref[...]).astype(bf16)
        store_grad(1, dot(mixed_two, back_two, ((0,), (0,))))
        store_grad(0, dot(mixed_one_ref[...], back_one, ((0,), (0,))))

    turns = {(stage, m): [] for stage in range(STAGES) for m in range(NZ - 1)}
    for m, dx, f in ((0, 0, 1), (1, 0, 0), (2, 1, 1), (3, 3, 0), (5, 2, 0), (6, 2, 1)):
        turns[1, m].append((0, dx, f))
    turns[2, 2].append((0, 1, 0))
    turns[2, 3].append((0, 3, 1))
    order = [(2, 0), (2, 1), (1, 1), (3, 0), (1, 0), (3, 1), (0, 1), (0, 0)]
    for stage in range(2, STAGES):
        for turn, (dx, f) in enumerate(order):
            turns[stage, min(turn, NZ - 2)].append((stage - 1, dx, f))

    for stage in range(STAGES):
        for m in range(NZ - 1):
            ring_tick(stage, m)
            if m == 5 and stage + 1 < STAGES:
                start_stage(stage + 1)
            if stage == 0:
                if m == 1:
                    send_tiles(range(blocks // 2, blocks))
                    copy_metas()
                if m in (2, 3, 4, 6):
                    build_table({2: (1, 0), 3: (3, 6), 4: (4, 5), 6: (2, 7)}[m])
                if m == 5:
                    pass_tiles(range(blocks // 2))
                continue
            if stage == 1:
                if m == 0:
                    for load in loads:
                        load.wait()
                    own_tiles.wait()
                    for i in range(blocks):
                        land(tile_slot(0, 1, i), t_sib.at[0, i])
                if m == 1:
                    pass_tiles(range(blocks // 2, blocks))
                if m == 2:
                    for i in range(blocks):
                        land(tile_slot(1, 1, i), t_sib.at[1, i])
                        land(tile_slot(NX - 1, 1, i), t_sib.at[NX - 1, i])
                if m == 5:
                    for i in range(blocks):
                        land(tile_slot(2, 0, i), t_far.at[i])
                        share_tiles(2, i)
                if m == 6:
                    for i in range(blocks):
                        land(tile_slot(2, 1, i), t_sib.at[2, i])
            for of, dx, f in turns[stage, m]:
                partial(of, dx * 2 + f)
        land(feat_slot(stage, 0, 1), sib_recv.at[stage])
        land(feat_slot(stage, 0, 0), own_sem.at[stage])
    last_partials()
    for stage in range(2):
        finish_one(stage)
    for i in range(blocks):
        build_local(i)
        layer_one(i)
    start_two()
    finish_two(2)
    finish_two(3)
    layer_two()

    half = width // 2
    quarter = half // NX
    part = quarter // NX
    place = ((my_x, my_y), (my_y, my_x))

    def rows_at(start, count):
        return pl.ds(pl.multiple_of(start, part), count)

    def along(h, turn, d):
        return (0, d, 0) if h == turn else (0, 0, 0, d)

    for h in range(2):
        here = pl.ds(h * half, half)
        remote(
            send_ref.at[other, here], pair_in.at[here], pair_send, pair_recv.at[h], (0, 0, 1)
        ).start()
    for h in range(2):
        here = pl.ds(h * half, half)
        land(pair_in.at[here], pair_recv.at[h])
        pair_sum[here, :] = (grad_ref[core, here, :] + pair_in[here, :].astype(f32)).astype(bf16)
        for d in (2, 1, 3):
            theirs = rows_at(h * half + lax.rem(place[h][0] + d, NX) * quarter, quarter)
            remote(
                pair_sum.at[theirs], first_in.at[h, NX - d - 1],
                first_send, first_recv.at[h], along(h, 0, d),
            ).start()
    for h in range(2):
        mine = rows_at(h * half + place[h][0] * quarter, quarter)
        value = grad_ref[core, mine, :] + pair_in[mine, :].astype(f32)
        land(first_in.at[h], first_recv.at[h])
        for n in range(NX - 1):
            value += first_in[h, n].astype(f32)
        first_sum[h] = value
        first_out[h] = value.astype(bf16)
        for d in (2, 1, 3):
            theirs = rows_at(lax.rem(place[h][1] + d, NX) * part, part)
            remote(
                first_out.at[h, theirs], second_in.at[h, NX - d - 1],
                second_send, second_recv.at[h], along(h, 1, d),
            ).start()
    tiles_of = [(r, q) for r in range(part // 8) for q in range(4)]
    for h in range(2):
        value = first_sum[h, rows_at(place[h][1] * part, part), :]
        land(second_in.at[h], second_recv.at[h])
        for n in range(NX - 1):
            value += second_in[h, n].astype(f32)
        for n, (r, q) in enumerate(tiles_of):
            third[n, h] = value[r * 8 : (r + 1) * 8, q * wide : (q + 1) * wide]
    for dz in (4, 3, 5, 2, 6, 1, 7):
        remote(
            third.at[lax.rem(my_z + dz, NZ)], third_in.at[NZ - dz - 1],
            third_send, third_recv, (dz, 0, 0),
        ).start()
    value = third[my_z]
    land(third_in, third_recv)
    for n in range(NZ - 1):
        value += third_in[n]
    third_done[my_z] = value
    for dz in (4, 3, 5, 2, 6, 1, 7):
        remote(
            third_done.at[my_z], third_done.at[my_z], done_send, done_recv, (dz, 0, 0)
        ).start()
    land(third_done.at[pl.ds(0, NZ - 1)], done_recv)

    for h in range(2):
        value = jnp.concatenate(
            [
                jnp.concatenate([third_done[r * 4 + q, h] for q in range(4)], axis=1)
                for r in range(part // 8)
            ],
            axis=0,
        )
        mine = rows_at(h * half + place[h][0] * quarter + place[h][1] * part, part)
        sum_ref[core, mine, :] = value.astype(bf16)
        for d in (2, 1, 3):
            remote(
                sum_ref.at[core, mine], sum_ref.at[core, mine],
                gather_send, gather_recv.at[h], along(h, 1, d),
            ).start()
    for h in range(2):
        land(second_in.at[h], gather_recv.at[h])
        mine = rows_at(h * half + place[h][0] * quarter, quarter)
        for d in (1, 3):
            remote(
                sum_ref.at[core, mine], sum_ref.at[core, mine],
                share_send, share_recv.at[h, NX - d - 1], along(h, 0, d),
            ).start()
        remote(
            sum_ref.at[core, mine], sum_ref.at[core, mine],
            back_send, back_recv.at[h, 0], (0, 0, 1),
        ).start()

    def share_at(h, d):
        return rows_at(h * half + lax.rem(place[h][0] + d, NX) * quarter, quarter)

    for d in (1, 3, 2):
        for h in range(2):
            got = share_at(h, d)
            land(sum_ref.at[core, got], share_recv.at[h, d - 1])
            if d != 2:
                start = h * half + lax.rem(place[h][0] + d, NX) * quarter
                piece = rows_at(start + (quarter // 2 if d == 1 else 0), quarter // 2)
                remote(
                    sum_ref.at[core, piece], sum_ref.at[core, piece],
                    share_send, share_recv.at[h, 1], along(h, 0, NX - d),
                ).start()
            remote(
                sum_ref.at[core, got], sum_ref.at[core, got],
                back_send, back_recv.at[h, d], (0, 0, 1),
            ).start()
    for d in range(NX):
        for h in range(2):
            land(sum_ref.at[other, share_at(h, d)], back_recv.at[h, d])

    for stage in range(STAGES):
        land(feats[stage].at[pl.ds(0, 15 * blocks)], z_send.at[stage])
        land(part_in.at[stage, pl.ds(1, 5)], p_send.at[stage])
        land(relay_in.at[stage], relay_send.at[stage])
    land(metas.at[pl.ds(1, len(near))], m_send)
    land(tiles_all.at[pl.ds(1, 2 * NX - 1)], t_send)
    land(pair_in, pair_send)
    land(first_in, first_send)
    land(second_in, second_send)
    land(third_in, third_send)
    land(third_in, done_send)
    land(second_in, gather_send)
    land(first_in, share_send)
    land(pair_in, back_send)


def layers(initial, history, tiles, cols, chosen, weight_one, weight_two, cotangent):
    blocks, size, width = initial.shape
    slots = tiles.shape[1]
    wide = width // 4
    rows = blocks * size
    quarter = width // 2 // NX
    part = quarter // NX
    vmem = pl.BlockSpec(memory_space=pltpu.VMEM)
    dma = pltpu.SemaphoreType.DMA
    bf16 = jnp.bfloat16
    f32 = jnp.float32
    metas = 2 * NX + 2 * (NZ - 1)
    return pl.pallas_call(
        layers_kernel,
        out_shape=(
            jax.ShapeDtypeStruct((rows, width), bf16),
            jax.ShapeDtypeStruct((2, width, width), bf16),
        ),
        in_specs=[vmem] * 5 + [pl.BlockSpec(memory_space=pl.ANY)] * 3,
        out_specs=(vmem, vmem),
        scratch_shapes=[pltpu.VMEM((width, width), bf16)] * 2
        + [pltpu.VMEM((rows, width), bf16), dma((3,))]
        + [pltpu.VMEM((2 * NZ * blocks + 1, size, wide), bf16)] * STAGES
        + [
            pltpu.VMEM((2 * NX, blocks, slots, size, size), bf16),
            pltpu.VMEM((STAGES, 2 * NX, blocks, size, wide), bf16),
            pltpu.VMEM((STAGES, 6, blocks, size, wide), bf16),
            pltpu.VMEM((STAGES, 2, blocks, size, wide), bf16),
            pltpu.VMEM((2, blocks, size, wide), f32),
            pltpu.VMEM((metas, 8, 128), jnp.int32),
            pltpu.SMEM((metas, 8, 128), jnp.int32),
            pltpu.SMEM((2 * NX * blocks * slots,), jnp.int32),
            pltpu.VMEM((rows, rows), bf16),
            pltpu.VMEM((4, rows, wide), f32),
            pltpu.VMEM((4, rows, wide), f32),
            pltpu.VMEM((rows, width), bf16),
            pltpu.VMEM((rows, width), bf16),
            pltpu.VMEM((rows, width), bf16),
            pltpu.VMEM((rows, width), f32),
            pltpu.VMEM((2, width, width), f32),
            pltpu.VMEM((2, width, width), bf16),
            pltpu.VMEM((width, width), bf16),
            pltpu.VMEM((width, width), bf16),
            pltpu.VMEM((2, NX - 1, quarter, width), bf16),
            pltpu.VMEM((2, quarter, width), f32),
            pltpu.VMEM((2, quarter, width), bf16),
            pltpu.VMEM((2, NX - 1, part, width), bf16),
            pltpu.VMEM((NZ, 2, 8, wide), f32),
            pltpu.VMEM((NZ - 1, 2, 8, wide), f32),
            pltpu.VMEM((NZ, 2, 8, wide), f32),
            dma((STAGES, 2, NZ - 1)),
            dma((STAGES,)),
            dma((STAGES,)),
            dma((STAGES,)),
            dma((2, blocks)),
            dma((blocks,)),
            dma((NX, blocks)),
            dma,
            dma,
            dma((STAGES,)),
            dma((STAGES,)),
            dma((STAGES, 2, blocks)),
            dma((STAGES,)),
            dma,
            dma,
            dma,
            dma,
            dma((2,)),
            dma,
            dma((2,)),
            dma,
            dma((2,)),
            dma,
            dma,
            dma,
            dma,
            dma,
            dma((2,)),
            dma,
            dma((2, NX - 1)),
            dma,
            dma((2, NX)),
        ],
        compiler_params=pltpu.CompilerParams(
            collective_id=0, has_side_effects=True, vmem_limit_bytes=56 * 2**20
        ),
        cost_estimate=pl.CostEstimate(
            flops=7 * 10**9, bytes_accessed=8 * 2**20, transcendentals=2**19
        ),
        name="layers",
    )(initial, history, tiles, cols, chosen, weight_one, weight_two, cotangent)


def finish_kernel(sum_ref, rows_ref, one_ref, two_ref, out_ref):
    one_ref[...] = BETA_ONE * sum_ref[0].astype(jnp.float32)
    two_ref[...] = BETA_TWO * sum_ref[1].astype(jnp.float32)
    out_ref[...] = rows_ref[...]


def finish(summed, output):
    width = summed.shape[1]
    rows = output.shape[0]
    steps = 2
    grad = pl.BlockSpec((width // steps, width), lambda n: (n, 0))
    out = pl.BlockSpec((rows // steps, width), lambda n: (n, 0))
    full = jax.ShapeDtypeStruct((width, width), jnp.float32)
    return pl.pallas_call(
        finish_kernel,
        grid=(steps,),
        out_shape=(full, full, jax.ShapeDtypeStruct(output.shape, output.dtype)),
        in_specs=[pl.BlockSpec((2, width // steps, width), lambda n: (0, n, 0)), out],
        out_specs=(grad, grad, out),
        compiler_params=pltpu.CompilerParams(vmem_limit_bytes=56 * 2**20),
        name="finish",
    )(summed, output)


def local(initial, history, tile_values, tile_cols, send_blocks, weight_one, weight_two, cotangent):
    tiles = tile_values[0]
    blocks, slots, size, _ = tiles.shape
    width = initial.shape[2]
    output, summed = layers(
        initial[0].reshape(blocks, size, width), history[0].reshape(blocks, size, width),
        tiles, tile_cols[0], send_blocks[0], weight_one, weight_two, cotangent[0],
    )
    grad_one, grad_two, output = finish(summed, output)
    return (output[None], grad_one, grad_two)


def solution(mesh):
    return jax.shard_map(
        local,
        mesh=mesh,
        in_specs=(
            P("grp", "dom", None),
            P("grp", "dom", None),
            P("grp", "dom", None, None, None),
            P("grp", "dom", None),
            P("grp", "dom", None),
            P(),
            P(),
            P("grp", "dom", None),
        ),
        out_specs=(P("grp", "dom", None), P(), P()),
        check_vma=False,
    )
```

```python
import functools

import jax
import jax.numpy as jnp
from jax import lax
from jax.experimental import pallas as pl
from jax.experimental.pallas import tpu as pltpu
from jax.sharding import PartitionSpec as P

RESTART = 0.1
BETA_ONE = 0.405465
BETA_TWO = 0.223144

NZ = 8
NX = 4
NY = 4
STAGES = 4
MESH = pl.DeviceIdType.MESH


def dom_index(z, x, core):
    return (z * NX + x) * 2 + core


def sigmoid(value):
    return 1.0 / (1.0 + jnp.exp(-value))


def dot(a, b, dims=((1,), (0,))):
    return lax.dot_general(a, b, (dims, ((), ())), preferred_element_type=jnp.float32)


def layers_kernel(
    initial_ref, history_any, tiles_ref, cols_ref, chosen_ref, one_any, two_any, cot_any,
    out_ref, sum_ref, history_ref, one_ref, two_ref, cot_ref, load_sem,
    feat0, feat1, feat2, feat3, tiles_all, part_out, part_in, relay_in, relay_sum, metas, metas_smem, table,
    local_ref, base_ref, received_ref, mixed_one_ref, mixed_two_ref, hidden_ref, slope_ref,
    grad_ref, send_ref, pair_in, pair_sum, first_in, first_sum, first_out, second_in,
    third, third_in, third_done,
    z_recv, sib_recv, z_send, own_sem, t_recv, t_far, t_sib, t_send, t_own, p_recv, p_send,
    relay_recv, relay_send, m_recv, m_send, m_copy, pair_send, pair_recv, first_send, first_recv,
    second_send, second_recv, third_send, third_recv, done_send, done_recv,
    gather_send, gather_recv, share_send, share_recv, back_send, back_recv,
):
    f32 = jnp.float32
    bf16 = jnp.bfloat16
    feats = (feat0, feat1, feat2, feat3)
    blocks, size, width = initial_ref.shape
    slots = tiles_ref.shape[1]
    wide = feat0.shape[2]
    rows = blocks * size
    dom = lax.axis_index("dom")
    my_y = lax.axis_index("grp")
    core = lax.rem(dom, 2)
    my_x = lax.rem(dom // 2, NX)
    my_z = dom // (2 * NX)
    other = 1 - core

    def at(dz, dx, flip, dy=0):
        z = lax.rem(my_z + dz, NZ)
        x = lax.rem(my_x + dx, NX)
        y = lax.rem(my_y + dy, NY)
        return (dom_index(z, x, other if flip else core), y)

    row = [(0, dx, f) for dx in range(NX) for f in range(2) if (dx, f) != (0, 0)]
    column = [(dz, 0, f) for dz in range(1, NZ) for f in range(2)]
    stack = [(0, 0, 0, dy) for dy in range(1, NY)]
    barrier = pltpu.get_barrier_semaphore()
    for peer in row + column + stack:
        pl.semaphore_signal(barrier, inc=1, device_id=at(*peer), device_id_type=MESH)
    pl.semaphore_wait(barrier, len(row) + len(column) + len(stack))

    def remote(src, dst, send_sem, recv_sem, peer):
        return pltpu.make_async_remote_copy(
            src_ref=src, dst_ref=dst, send_sem=send_sem, recv_sem=recv_sem,
            device_id=at(*peer), device_id_type=MESH,
        )

    def land(ref, sem):
        pltpu.make_async_copy(ref, ref, sem).wait()

    def feat_slot(stage, dz, flip):
        return feats[stage].at[pl.ds((dz * 2 + flip) * blocks, blocks)]

    def own_columns(stage, flip):
        ref = (initial_ref, history_ref)[stage // 2]
        half = other if flip else core
        start = pl.multiple_of((half * 2 + stage % 2) * wide, wide)
        return ref.at[:, :, pl.ds(start, wide)]

    def start_stage(stage):
        for flip in range(2):
            for direction, dz in ((0, 1), (1, NZ - 1)):
                remote(
                    own_columns(stage, flip), feat_slot(stage, NZ - dz, flip),
                    z_send.at[stage], z_recv.at[stage, direction, flip], (dz, 0, flip),
                ).start()
        remote(
            own_columns(stage, 1), feat_slot(stage, 0, 1),
            z_send.at[stage], sib_recv.at[stage], (0, 0, 1),
        ).start()
        pltpu.make_async_copy(own_columns(stage, 0), feat_slot(stage, 0, 0), own_sem.at[stage]).start()

    def ring_tick(stage, m):
        for direction, dz in ((0, 1), (1, NZ - 1)):
            hop = m // 2 + 1
            flip = m % 2 if hop < NZ // 2 else direction
            origin = (NZ - hop if direction == 0 else hop) % NZ
            slot = feat_slot(stage, origin, flip)
            land(slot, z_recv.at[stage, direction, m])
            if hop < NZ // 2 - 1 or (hop == NZ // 2 - 1 and flip == direction):
                later = m + 2 if hop < NZ // 2 - 1 else NZ - 2
                next_origin = (NZ - hop - 1 if direction == 0 else hop + 1) % NZ
                remote(
                    slot, feat_slot(stage, next_origin, flip),
                    z_send.at[stage], z_recv.at[stage, direction, later], (dz, 0, 0),
                ).start()

    def tile_slot(dx, flip, i):
        return tiles_all.at[dx * 2 + flip, i]

    def send_tiles(which):
        for n in which:
            for i, dx, sem in ((n, 1, 0), (blocks - 1 - n, NX - 1, 1)):
                remote(
                    tiles_ref.at[i], tile_slot(NX - dx, 0, i), t_send, t_recv.at[sem, i], (0, dx, 0)
                ).start()

    def share_tiles(dx, i):
        remote(
            tile_slot(dx, 0, i), tile_slot(dx, 1, i), t_send, t_sib.at[dx, i], (0, 0, 1)
        ).start()

    def pass_tiles(which):
        for n in which:
            for i, dx, sem in ((n, NX - 1, 0), (blocks - 1 - n, 1, 1)):
                land(tile_slot(dx, 0, i), t_recv.at[sem, i])
                if n < blocks // 2:
                    toward = 1 if sem == 0 else NX - 1
                    remote(
                        tile_slot(dx, 0, i), tile_slot(2, 0, i), t_send, t_far.at[i], (0, toward, 0)
                    ).start()
                share_tiles(dx, i)

    near = [(0, 0, 1)] + [p for p in row if p[1] != 0] + column
    metas[0, pl.ds(0, blocks), pl.ds(0, slots)] = cols_ref[...]
    metas[0, pl.ds(blocks, 1), pl.ds(0, chosen_ref.shape[1])] = chosen_ref[...]
    start_stage(0)
    for peer in near:
        dz, dx, f = peer
        if dz == 0:
            slot = ((NX - dx) % NX) * 2 + f
        else:
            slot = 2 * NX + (NZ - dz - 1) * 2 + f
        remote(metas.at[0], metas.at[slot], m_send, m_recv, peer).start()
    for i in range(blocks):
        remote(tiles_ref.at[i], tile_slot(0, 1, i), t_send, t_sib.at[0, i], (0, 0, 1)).start()
    loads = [
        pltpu.make_async_copy(src, dst, load_sem.at[n])
        for n, (src, dst) in enumerate(((one_any, one_ref), (two_any, two_ref), (cot_any, cot_ref), (history_any, history_ref)))
    ]
    for load in loads:
        load.start()
    send_tiles(range(blocks // 2))
    own_tiles = pltpu.make_async_copy(tiles_ref, tiles_all.at[0], t_own)
    own_tiles.start()
    for f in feats:
        f[2 * NZ * blocks] = jnp.zeros((size, wide), f.dtype)

    def copy_metas():
        land(metas.at[pl.ds(1, len(near))], m_recv)
        copy = pltpu.make_async_copy(metas, metas_smem, m_copy)
        copy.start()
        copy.wait()

    def build_table(readers):
        for reader in readers:
            dx, f = reader // 2, reader % 2
            reader_index = dom_index(my_z, lax.rem(my_x + dx, NX), other if f else core)

            def entry(n, carry):
                col = metas_smem[reader, lax.div(n, slots), lax.rem(n, slots)]
                owner = jnp.maximum(col - blocks, 0)
                chip = lax.div(owner, 2)
                valid = (col >= blocks) & (lax.rem(chip, NX) == my_x)
                dz = lax.rem(lax.div(chip, NX) + (NZ - my_z), NZ)
                flip = lax.rem(owner + core, 2)
                place = dz * 2 + flip
                where = jnp.where(dz == 0, flip, place + (2 * NX - 2))
                block = metas_smem[where, blocks, reader_index]
                slot = place * blocks + block
                table[reader * blocks * slots + n] = jnp.where(valid, slot, 2 * NZ * blocks)
                return carry

            lax.fori_loop(0, blocks * slots, entry, 0, unroll=slots)

    def build_local(i):
        sums = [jnp.zeros((size, size), f32) for _ in range(blocks)]
        for k in range(slots):
            tile = tiles_all[0, i, k].astype(f32)
            for c in range(blocks):
                mask = jnp.where(metas_smem[0, i, k] == c, 1.0, 0.0).astype(f32)
                sums[c] += tile * mask
        for c in range(blocks):
            local_ref[pl.ds(i * size, size), pl.ds(c * size, size)] = sums[c].astype(bf16)

    def product(stage, reader, i):
        first = (reader * blocks + i) * slots
        left = jnp.concatenate([tiles_all[reader, i, k] for k in range(slots)], axis=1)
        right = jnp.concatenate([feats[stage][table[first + k]] for k in range(slots)], axis=0)
        return dot(left, right)

    def send_part(stage, reader, which=slice(None)):
        dx, f = reader // 2, reader % 2
        if dx == 2:
            toward = 1 if f == 0 else NX - 1
            remote(
                part_out.at[stage, reader, which], relay_in.at[stage, f, which],
                relay_send.at[stage], relay_recv.at[stage, f, 0 if which == slice(None) else which],
                (0, toward, 0),
            ).start()
        elif reader:
            source = {0: 0, 1: 2, NX - 1: 1}[dx]
            remote(
                part_out.at[stage, reader, which], part_in.at[stage, source * 2 + f, which],
                p_send.at[stage], p_recv.at[stage], (0, dx, f),
            ).start()

    def partial(stage, reader):
        dx, f = reader // 2, reader % 2
        relays = (dx, f) in ((1, 0), (NX - 1, 1))
        if relays:
            land(relay_in.at[stage, f], relay_recv.at[stage, f, 0])

        def one(i, carry):
            total = product(stage, reader, i)
            if relays:
                total += relay_in[stage, f, i].astype(f32)
            part_out[stage, reader, i] = total.astype(bf16)
            return carry

        lax.fori_loop(0, blocks, one, 0, unroll=blocks)
        send_part(stage, reader)

    def last_partials():
        stage = STAGES - 1
        for reader in (4, 5, 3, 6):
            totals = [product(stage, reader, i) for i in range(blocks)]
            for i in range(blocks):
                part_out[stage, reader, i] = totals[i].astype(bf16)
            if reader // 2 == 2:
                for i in range(blocks):
                    send_part(stage, reader, i)
            else:
                send_part(stage, reader)
        relayed = (2, 7)
        for reader in relayed:
            for i in range(blocks):
                relay_sum[reader % 2, i] = product(stage, reader, i)
        for i in range(blocks):
            for reader in relayed:
                f = reader % 2
                land(relay_in.at[stage, f, i], relay_recv.at[stage, f, i])
                total = relay_sum[f, i] + relay_in[stage, f, i].astype(f32)
                part_out[stage, reader, i] = total.astype(bf16)
                send_part(stage, reader, i)
        for reader in (1, 0):
            for i in range(blocks):
                part_out[stage, reader, i] = product(stage, reader, i).astype(bf16)
            send_part(stage, reader)

    def column_chunk(stage, flip):
        return (other if flip else core) * 2 + stage % 2

    def total_of(stage, flip):
        first = part_in[stage, 1] if flip else part_out[stage, 0]
        total = first.astype(f32)
        for source in (1, 2):
            total += part_in[stage, source * 2 + flip].astype(f32)
        return total.reshape(rows, wide)

    def received(stage):
        land(part_in.at[stage, pl.ds(1, 5)], p_recv.at[stage])

    def finish_one(stage):
        received(stage)
        for flip in range(2):
            received_ref[column_chunk(stage, flip)] = total_of(stage, flip)

    def layer_one(i):
        here = pl.ds(i * size, size)
        local = local_ref[here, :]
        own = initial_ref[...].reshape(rows, width)
        got = jnp.concatenate([received_ref[q, here, :] for q in range(4)], axis=1)
        mixed = (
            (1.0 - RESTART) * (dot(local, own) + got) + RESTART * initial_ref[i].astype(f32)
        ).astype(bf16)
        pre = (1.0 - BETA_ONE) * mixed.astype(f32) + BETA_ONE * dot(mixed, one_ref[...])
        sig = sigmoid(pre)
        mixed_one_ref[here, :] = mixed
        hidden_ref[here, :] = (pre * sig).astype(bf16)
        slope_ref[here, :] = sig * (1.0 + pre * (1.0 - sig))

    def start_two():
        total = (1.0 - RESTART) * dot(local_ref[...], hidden_ref[...]) + RESTART * initial_ref[
            ...
        ].reshape(rows, width).astype(f32)
        for q in range(4):
            base_ref[q] = total[:, q * wide : (q + 1) * wide]

    def finish_two(stage):
        received(stage)
        for flip in range(2):
            chunk = column_chunk(stage, flip)
            mixed = base_ref[chunk] + (1.0 - RESTART) * total_of(stage, flip)
            mixed_two_ref[:, pl.ds(pl.multiple_of(chunk * wide, wide), wide)] = mixed.astype(bf16)

    def store_grad(g, grad):
        grad_ref[g] = grad
        send_ref[g] = grad.astype(bf16)

    def layer_two():
        mixed_two = mixed_two_ref[...]
        pre_two = (1.0 - BETA_TWO) * mixed_two.astype(f32) + BETA_TWO * dot(mixed_two, two_ref[...])
        sig = sigmoid(pre_two)
        out_ref[...] = (pre_two * sig).astype(bf16)
        slope_two = sig * (1.0 + pre_two * (1.0 - sig))
        back_two = (cot_ref[...].astype(f32) * slope_two).astype(bf16)
        back_mixed = (
            (1.0 - BETA_TWO) * back_two.astype(f32)
            + BETA_TWO * dot(back_two, two_ref[...], ((1,), (1,)))
        ).astype(bf16)
        back_hidden = (1.0 - RESTART) * dot(local_ref[...], back_mixed, ((0,), (0,)))
        back_one = (back_hidden * slope_ref[...]).astype(bf16)
        store_grad(1, dot(mixed_two, back_two, ((0,), (0,))))
        store_grad(0, dot(mixed_one_ref[...], back_one, ((0,), (0,))))

    turns = {(stage, m): [] for stage in range(STAGES) for m in range(NZ - 1)}
    for m, dx, f in ((0, 0, 1), (1, 0, 0), (2, 1, 1), (3, 3, 0), (5, 2, 0), (6, 2, 1)):
        turns[1, m].append((0, dx, f))
    turns[2, 2].append((0, 1, 0))
    turns[2, 3].append((0, 3, 1))
    order = [(2, 0), (2, 1), (1, 1), (3, 0), (1, 0), (3, 1), (0, 1), (0, 0)]
    for stage in range(2, STAGES):
        for turn, (dx, f) in enumerate(order):
            turns[stage, min(turn, NZ - 2)].append((stage - 1, dx, f))

    for stage in range(STAGES):
        for m in range(NZ - 1):
            ring_tick(stage, m)
            if m == 5 and stage + 1 < STAGES:
                start_stage(stage + 1)
            if stage == 0:
                if m == 1:
                    send_tiles(range(blocks // 2, blocks))
                    copy_metas()
                if m in (2, 3, 4, 6):
                    build_table({2: (1, 0), 3: (3, 6), 4: (4, 5), 6: (2, 7)}[m])
                if m == 5:
                    pass_tiles(range(blocks // 2))
                continue
            if stage == 1:
                if m == 0:
                    for load in loads:
                        load.wait()
                    own_tiles.wait()
                    for i in range(blocks):
                        land(tile_slot(0, 1, i), t_sib.at[0, i])
                if m == 1:
                    pass_tiles(range(blocks // 2, blocks))
                if m == 2:
                    for i in range(blocks):
                        land(tile_slot(1, 1, i), t_sib.at[1, i])
                        land(tile_slot(NX - 1, 1, i), t_sib.at[NX - 1, i])
                if m == 5:
                    for i in range(blocks):
                        land(tile_slot(2, 0, i), t_far.at[i])
                        share_tiles(2, i)
                if m == 6:
                    for i in range(blocks):
                        land(tile_slot(2, 1, i), t_sib.at[2, i])
            for of, dx, f in turns[stage, m]:
                partial(of, dx * 2 + f)
        land(feat_slot(stage, 0, 1), sib_recv.at[stage])
        land(feat_slot(stage, 0, 0), own_sem.at[stage])
    last_partials()
    for stage in range(2):
        finish_one(stage)
    for i in range(blocks):
        build_local(i)
        layer_one(i)
    start_two()
    finish_two(2)
    finish_two(3)
    layer_two()

    half = width // 2
    quarter = half // NX
    part = quarter // NX
    place = ((my_x, my_y), (my_y, my_x))

    def rows_at(start, count):
        return pl.ds(pl.multiple_of(start, part), count)

    def along(h, turn, d):
        return (0, d, 0) if h == turn else (0, 0, 0, d)

    for h in range(2):
        here = pl.ds(h * half, half)
        remote(
            send_ref.at[other, here], pair_in.at[here], pair_send, pair_recv.at[h], (0, 0, 1)
        ).start()
    for h in range(2):
        here = pl.ds(h * half, half)
        land(pair_in.at[here], pair_recv.at[h])
        pair_sum[here, :] = (grad_ref[core, here, :] + pair_in[here, :].astype(f32)).astype(bf16)
        for d in (2, 1, 3):
            theirs = rows_at(h * half + lax.rem(place[h][0] + d, NX) * quarter, quarter)
            remote(
                pair_sum.at[theirs], first_in.at[h, NX - d - 1],
                first_send, first_recv.at[h], along(h, 0, d),
            ).start()
    for h in range(2):
        mine = rows_at(h * half + place[h][0] * quarter, quarter)
        value = grad_ref[core, mine, :] + pair_in[mine, :].astype(f32)
        land(first_in.at[h], first_recv.at[h])
        for n in range(NX - 1):
            value += first_in[h, n].astype(f32)
        first_sum[h] = value
        first_out[h] = value.astype(bf16)
        for d in (2, 1, 3):
            theirs = rows_at(lax.rem(place[h][1] + d, NX) * part, part)
            remote(
                first_out.at[h, theirs], second_in.at[h, NX - d - 1],
                second_send, second_recv.at[h], along(h, 1, d),
            ).start()
    tiles_of = [(r, q) for r in range(part // 8) for q in range(4)]
    for h in range(2):
        value = first_sum[h, rows_at(place[h][1] * part, part), :]
        land(second_in.at[h], second_recv.at[h])
        for n in range(NX - 1):
            value += second_in[h, n].astype(f32)
        for n, (r, q) in enumerate(tiles_of):
            third[n, h] = value[r * 8 : (r + 1) * 8, q * wide : (q + 1) * wide]
    for dz in (4, 3, 5, 2, 6, 1, 7):
        remote(
            third.at[lax.rem(my_z + dz, NZ)], third_in.at[NZ - dz - 1],
            third_send, third_recv, (dz, 0, 0),
        ).start()
    value = third[my_z]
    land(third_in, third_recv)
    for n in range(NZ - 1):
        value += third_in[n]
    third_done[my_z] = value
    for dz in (4, 3, 5, 2, 6, 1, 7):
        remote(
            third_done.at[my_z], third_done.at[my_z], done_send, done_recv, (dz, 0, 0)
        ).start()
    land(third_done.at[pl.ds(0, NZ - 1)], done_recv)

    for h in range(2):
        value = jnp.concatenate(
            [
                jnp.concatenate([third_done[r * 4 + q, h] for q in range(4)], axis=1)
                for r in range(part // 8)
            ],
            axis=0,
        )
        mine = rows_at(h * half + place[h][0] * quarter + place[h][1] * part, part)
        sum_ref[core, mine, :] = value.astype(bf16)
        for d in (2, 1, 3):
            remote(
                sum_ref.at[core, mine], sum_ref.at[core, mine],
                gather_send, gather_recv.at[h], along(h, 1, d),
            ).start()
    for h in range(2):
        land(second_in.at[h], gather_recv.at[h])
        mine = rows_at(h * half + place[h][0] * quarter, quarter)
        for d in (2, 1, 3):
            remote(
                sum_ref.at[core, mine], sum_ref.at[core, mine],
                share_send, share_recv.at[h, NX - d - 1], along(h, 0, d),
            ).start()
        remote(
            sum_ref.at[core, mine], sum_ref.at[core, mine],
            back_send, back_recv.at[h, 0], (0, 0, 1),
        ).start()

    def share_at(h, d):
        return rows_at(h * half + lax.rem(place[h][0] + d, NX) * quarter, quarter)

    for d in (1, 3, 2):
        for h in range(2):
            got = share_at(h, d)
            land(sum_ref.at[core, got], share_recv.at[h, d - 1])
            remote(
                sum_ref.at[core, got], sum_ref.at[core, got],
                back_send, back_recv.at[h, d], (0, 0, 1),
            ).start()
    for d in range(NX):
        for h in range(2):
            land(sum_ref.at[other, share_at(h, d)], back_recv.at[h, d])

    for stage in range(STAGES):
        land(feats[stage].at[pl.ds(0, 15 * blocks)], z_send.at[stage])
        land(part_in.at[stage, pl.ds(1, 5)], p_send.at[stage])
        land(relay_in.at[stage], relay_send.at[stage])
    land(metas.at[pl.ds(1, len(near))], m_send)
    land(tiles_all.at[pl.ds(1, 2 * NX - 1)], t_send)
    land(pair_in, pair_send)
    land(first_in, first_send)
    land(second_in, second_send)
    land(third_in, third_send)
    land(third_in, done_send)
    land(second_in, gather_send)
    land(first_in, share_send)
    land(pair_in, back_send)


def layers(initial, history, tiles, cols, chosen, weight_one, weight_two, cotangent):
    blocks, size, width = initial.shape
    slots = tiles.shape[1]
    wide = width // 4
    rows = blocks * size
    quarter = width // 2 // NX
    part = quarter // NX
    vmem = pl.BlockSpec(memory_space=pltpu.VMEM)
    far = pl.BlockSpec(memory_space=pl.ANY)
    dma = pltpu.SemaphoreType.DMA
    bf16 = jnp.bfloat16
    f32 = jnp.float32
    metas = 2 * NX + 2 * (NZ - 1)
    return pl.pallas_call(
        layers_kernel,
        out_shape=(
            jax.ShapeDtypeStruct((rows, width), bf16),
            jax.ShapeDtypeStruct((2, width, width), bf16),
        ),
        in_specs=[vmem, far, far, vmem, vmem, far, far, far],
        out_specs=(vmem, vmem),
        scratch_shapes=[pltpu.VMEM((blocks, size, width), bf16)]
        + [pltpu.VMEM((width, width), bf16)] * 2
        + [pltpu.VMEM((rows, width), bf16), dma((4,))]
        + [pltpu.VMEM((2 * NZ * blocks + 1, size, wide), bf16)] * STAGES
        + [
            pltpu.VMEM((2 * NX, blocks, slots, size, size), bf16),
            pltpu.VMEM((STAGES, 2 * NX, blocks, size, wide), bf16),
            pltpu.VMEM((STAGES, 6, blocks, size, wide), bf16),
            pltpu.VMEM((STAGES, 2, blocks, size, wide), bf16),
            pltpu.VMEM((2, blocks, size, wide), f32),
            pltpu.VMEM((metas, 8, 128), jnp.int32),
            pltpu.SMEM((metas, 8, 128), jnp.int32),
            pltpu.SMEM((2 * NX * blocks * slots,), jnp.int32),
            pltpu.VMEM((rows, rows), bf16),
            pltpu.VMEM((4, rows, wide), f32),
            pltpu.VMEM((4, rows, wide), f32),
            pltpu.VMEM((rows, width), bf16),
            pltpu.VMEM((rows, width), bf16),
            pltpu.VMEM((rows, width), bf16),
            pltpu.VMEM((rows, width), f32),
            pltpu.VMEM((2, width, width), f32),
            pltpu.VMEM((2, width, width), bf16),
            pltpu.VMEM((width, width), bf16),
            pltpu.VMEM((width, width), bf16),
            pltpu.VMEM((2, NX - 1, quarter, width), bf16),
            pltpu.VMEM((2, quarter, width), f32),
            pltpu.VMEM((2, quarter, width), bf16),
            pltpu.VMEM((2, NX - 1, part, width), bf16),
            pltpu.VMEM((NZ, 2, 8, wide), f32),
            pltpu.VMEM((NZ - 1, 2, 8, wide), f32),
            pltpu.VMEM((NZ, 2, 8, wide), f32),
            dma((STAGES, 2, NZ - 1)),
            dma((STAGES,)),
            dma((STAGES,)),
            dma((STAGES,)),
            dma((2, blocks)),
            dma((blocks,)),
            dma((NX, blocks)),
            dma,
            dma,
            dma((STAGES,)),
            dma((STAGES,)),
            dma((STAGES, 2, blocks)),
            dma((STAGES,)),
            dma,
            dma,
            dma,
            dma,
            dma((2,)),
            dma,
            dma((2,)),
            dma,
            dma((2,)),
            dma,
            dma,
            dma,
            dma,
            dma,
            dma((2,)),
            dma,
            dma((2, NX - 1)),
            dma,
            dma((2, NX)),
        ],
        compiler_params=pltpu.CompilerParams(
            collective_id=0, has_side_effects=True, vmem_limit_bytes=56 * 2**20
        ),
        cost_estimate=pl.CostEstimate(
            flops=7 * 10**9, bytes_accessed=8 * 2**20, transcendentals=2**19
        ),
        name="layers",
    )(initial, history, tiles, cols, chosen, weight_one, weight_two, cotangent)


def finish_kernel(sum_ref, rows_ref, one_ref, two_ref, out_ref):
    one_ref[...] = BETA_ONE * sum_ref[0].astype(jnp.float32)
    two_ref[...] = BETA_TWO * sum_ref[1].astype(jnp.float32)
    out_ref[...] = rows_ref[...]


def finish(summed, output):
    width = summed.shape[1]
    rows = output.shape[0]
    steps = 2
    grad = pl.BlockSpec((width // steps, width), lambda n: (n, 0))
    out = pl.BlockSpec((rows // steps, width), lambda n: (n, 0))
    full = jax.ShapeDtypeStruct((width, width), jnp.float32)
    return pl.pallas_call(
        finish_kernel,
        grid=(steps,),
        out_shape=(full, full, jax.ShapeDtypeStruct(output.shape, output.dtype)),
        in_specs=[pl.BlockSpec((2, width // steps, width), lambda n: (0, n, 0)), out],
        out_specs=(grad, grad, out),
        compiler_params=pltpu.CompilerParams(vmem_limit_bytes=56 * 2**20),
        name="finish",
    )(summed, output)


def local(initial, history, tile_values, tile_cols, send_blocks, weight_one, weight_two, cotangent):
    tiles = tile_values[0]
    blocks, slots, size, _ = tiles.shape
    width = initial.shape[2]
    output, summed = layers(
        initial[0].reshape(blocks, size, width), history[0].reshape(blocks, size, width),
        tiles, tile_cols[0], send_blocks[0], weight_one, weight_two, cotangent[0],
    )
    grad_one, grad_two, output = finish(summed, output)
    return (output[None], grad_one, grad_two)


def solution(mesh):
    return jax.shard_map(
        local,
        mesh=mesh,
        in_specs=(
            P("grp", "dom", None),
            P("grp", "dom", None),
            P("grp", "dom", None, None, None),
            P("grp", "dom", None),
            P("grp", "dom", None),
            P(),
            P(),
            P("grp", "dom", None),
        ),
        out_specs=(P("grp", "dom", None), P(), P()),
        check_vma=False,
    )
```
